32 devices in a mesh: row: 8 (over z, core), col: 4 (over y, x).
Axes of the slice: x: 2, y: 2, z: 4, core: 2. Of those that a mesh axis runs over, the one named last changes fastest.
Arguments:
- centroids: float32 [3, 1024], P(None, ('row', 'col')), may hold values from -4 to 4
- strengths: float32 [32, 1024], P(None, ('row', 'col')), may hold values from -6 to 6
- self_inv: float32 [32, 1024], P(None, ('row', 'col')), may hold values from -6 to 6
- wavenumbers: float32 [16], replicated, may hold values from 0.3 to 2
- field_pos: float32 [3, 2048], P(None, 'row'), may hold values from -4 to 4
- targets: float32 [32, 2048], P(None, 'row'), may hold values from -6 to 6
- lists: int32 [2048, 64], P('row'), may hold values from 0 to 1023
- connect: int32 [4, 1024], P(None, 'row'), may hold values from 0 to 1023, as said below
Outputs:
- adjoint: float32 [32, 1024], P(None, ('row', 'col'))
- vertex_sens: float32 [3, 1024], P(None, ('row', 'col'))
- objective: float32 [], replicated
The draws below stay inside these ranges and needn't reach their ends.
Inputs may be any that keep to these rules, and one draw needn't show every extreme that they name: `connect`: the four vertices of panel i lie in the block of 128 vertices that starts at i - i % 128; the first of them is i itself.
All inputs are finite; a program needn't handle non-finite values.
Results may differ from the reference program's by a relative error of at most 0.0003.
Values sent between devices are 32-bit elements; how exact they have to be, the bound alone decides.
A program may use at most 64 MiB of HBM per device.

```python
import math
import jax
import jax.numpy as jnp
import numpy as np
from jax import lax

PAN_DEV = 32
NF = 16
LIST = 64
PANELS = 1024
VERTS = 1024
ROWBLOCK = 128
FIELD = 2048


def draw_connect(key, part):
    panel_index = jnp.arange(PANELS, dtype=jnp.int32)
    inside = panel_index % ROWBLOCK
    start = panel_index - inside
    steps = jax.random.randint(key, (4, PANELS), 0, 2 * PAN_DEV + 1, dtype=jnp.int32)
    corner_index = jnp.arange(4, dtype=jnp.int32)[:, None]
    steps = jnp.where(corner_index == 0, jnp.zeros_like(steps), steps)
    return start[None, :] + (inside[None, :] + steps) % ROWBLOCK


def plant(result, key, smallest, top_value):
    extent = result.shape
    spot = [jax.random.randint(jax.random.fold_in(key, axis), (), 0, extent[axis]) for axis in range(len(extent))]
    result = result.at[tuple(spot)].set(smallest)
    longest = extent.index(max(extent))
    spot[longest] = (spot[longest] + 1) % extent[longest]
    return result.at[tuple(spot)].set(top_value)


def levels(stream_key, shape, pieces, smallest, high):
    gain, own = 1.0, jax.random.fold_in(stream_key, 6)
    for position, blocks in pieces:
        heights = jnp.exp(jax.random.uniform(jax.random.fold_in(own, position), (blocks,), jnp.float32, smallest / len(pieces), high / len(pieces)))
        gain = gain * jnp.repeat(heights, shape[position] // blocks).reshape([-1 if axis == position else 1 for axis in range(len(shape))])
    return gain


def rank_bounds(number_of, skew):
    weights = [(1 << 20) // math.isqrt(rank ** skew) + 1 for rank in range(1, number_of + 1)]
    spread = 1 + sum(weights) // (1 << 30)
    return np.cumsum(np.array([max(1, weight // spread) for weight in weights]))


def ranked(key, extent, number_of, slope):
    table = rank_bounds(number_of, slope)
    pick = jax.random.randint(jax.random.fold_in(key, 1), extent, 0, int(table[number_of - 1]))
    grade = jnp.searchsorted(jnp.asarray(table, jnp.int32), pick, side="right")
    return jax.random.permutation(jax.random.fold_in(key, 2), number_of)[grade].astype(jnp.int32)


def noise(key, extent, scale, bound, split=(), kind=jnp.bfloat16):
    array = scale * jax.random.normal(key, extent, jnp.float32)
    if split:
        array = array * levels(key, extent, split, -0.22, 0.18)
    return jnp.clip(array, -bound, bound).astype(kind)


def setup_inputs(seed: int = 0) -> dict:
    arg_keys = jax.random.split(jax.random.key(seed), 9)
    centroids = jnp.clip(jax.random.uniform(arg_keys[0], (3, PANELS), jnp.float32, -4.0, 4.0) * levels(arg_keys[0], (3, PANELS), ((1, 32),), -0.4, 0.0), -4.0, 4.0)
    strengths = noise(arg_keys[1], (2 * NF, PANELS), 1.0, 6.0, ((1, 32),), jnp.float32)
    self_inv = noise(arg_keys[2], (2 * NF, PANELS), 1.0, 6.0, ((1, 32),), jnp.float32)
    wavenumbers = jnp.clip(jnp.exp(jax.random.uniform(arg_keys[3], (NF,), jnp.float32, math.log(0.3), math.log(2.0))), 0.3, 2.0)
    field_pos = jnp.clip(jax.random.uniform(arg_keys[4], (3, FIELD), jnp.float32, -4.0, 4.0) * levels(arg_keys[4], (3, FIELD), ((1, 8),), -0.4, 0.0), -4.0, 4.0)
    targets = noise(arg_keys[5], (2 * NF, FIELD), 1.0, 6.0, ((1, 8),), jnp.float32)
    lists = plant(ranked(arg_keys[6], (FIELD, LIST), PANELS, 2), jax.random.fold_in(arg_keys[6], 3), 0, PANELS - 1).astype(jnp.int32)
    connect = draw_connect(jax.random.fold_in(arg_keys[8], 71), 0)
    return {"centroids": centroids, "strengths": strengths, "self_inv": self_inv, "wavenumbers": wavenumbers, "field_pos": field_pos, "targets": targets, "lists": lists, "connect": connect}


SOFT = 1.0

def pair_block(target_pos, target_str, target_mu, source_pos, source_str, source_mu, wavenumbers):
    freqs = wavenumbers.shape[0]
    offset = target_pos[:, None, :] - source_pos[:, :, None]
    squared = lax.optimization_barrier(jnp.sum(offset * offset, axis=0)) + SOFT
    inverse = lax.rsqrt(squared)
    distance = squared * inverse
    inverse_sq = inverse * inverse
    phase = wavenumbers[:, None, None] * distance[None]
    cosine = jnp.cos(phase)
    sine = jnp.sin(phase)
    deriv_real = -(cosine + phase * sine) * inverse_sq
    deriv_imag = (phase * cosine - sine) * inverse_sq
    tgt_real = target_str[:freqs, None, :]
    tgt_imag = target_str[freqs:, None, :]
    tmu_real = target_mu[:freqs, None, :]
    tmu_imag = target_mu[freqs:, None, :]
    src_real = source_str[:freqs, :, None]
    src_imag = source_str[freqs:, :, None]
    smu_real = source_mu[:freqs, :, None]
    smu_imag = source_mu[freqs:, :, None]
    prod_real = tmu_real * src_real - tmu_imag * src_imag + smu_real * tgt_real - smu_imag * tgt_imag
    prod_imag = tmu_real * src_imag + tmu_imag * src_real + smu_real * tgt_imag + smu_imag * tgt_real
    weight = lax.optimization_barrier(jnp.sum(prod_real * deriv_real - prod_imag * deriv_imag, axis=0)) * inverse
    return lax.optimization_barrier(jnp.sum(weight[None] * offset, axis=1))

def reference(centroids, strengths, self_inv, wavenumbers, field_pos, targets, lists, connect):
    panel_ids = lists.reshape(-1)
    near = centroids[:, panel_ids]
    observer = jnp.repeat(field_pos, LIST, axis=1)
    offset = observer - near
    distance = jnp.sqrt(lax.optimization_barrier(jnp.sum(offset * offset, axis=0)) + SOFT)
    inverse = 1.0 / distance
    phase = wavenumbers[:, None] * distance[None]
    cosine = jnp.cos(phase)
    sine = jnp.sin(phase)
    str_real = strengths[:NF][:, panel_ids]
    str_imag = strengths[NF:][:, panel_ids]
    part_real = (cosine * str_real - sine * str_imag) * inverse
    part_imag = (cosine * str_imag + sine * str_real) * inverse
    eta_real = part_real.reshape(NF, FIELD, LIST).sum(axis=2)
    eta_imag = part_imag.reshape(NF, FIELD, LIST).sum(axis=2)
    res_real = eta_real - targets[:NF]
    res_imag = eta_imag - targets[NF:]
    objective = (jnp.sum(res_real * res_real) + jnp.sum(res_imag * res_imag)) / (NF * FIELD) + 1e-06
    rep_real = jnp.repeat(res_real, LIST, axis=1)
    rep_imag = jnp.repeat(res_imag, LIST, axis=1)
    term_real = (cosine * rep_real + sine * rep_imag) * inverse
    term_imag = (cosine * rep_imag - sine * rep_real) * inverse
    src_real = jnp.zeros((NF, PANELS), jnp.float32).at[:, panel_ids].add(term_real) / objective
    src_imag = jnp.zeros((NF, PANELS), jnp.float32).at[:, panel_ids].add(term_imag) / objective
    inv_real = self_inv[:NF]
    inv_imag = self_inv[NF:]
    adjoint = jnp.concatenate([src_real * inv_real - src_imag * inv_imag, src_real * inv_imag + src_imag * inv_real], axis=0)
    width = math.gcd(PANELS, 256)
    count = PANELS // width

    def one_target(start):
        tpos = lax.dynamic_slice_in_dim(centroids, start, width, 1)
        tstr = lax.dynamic_slice_in_dim(strengths, start, width, 1)
        tmu = lax.dynamic_slice_in_dim(adjoint, start, width, 1)

        def visit_block(total, sstart):
            spos = lax.dynamic_slice_in_dim(centroids, sstart, width, 1)
            sstr = lax.dynamic_slice_in_dim(strengths, sstart, width, 1)
            smu = lax.dynamic_slice_in_dim(adjoint, sstart, width, 1)
            return (total + pair_block(tpos, tstr, tmu, spos, sstr, smu, wavenumbers), None)
        total, _ = lax.scan(visit_block, jnp.zeros((3, width), jnp.float32), jnp.arange(count, dtype=jnp.int32) * width)
        return total
    blocks = lax.map(one_target, jnp.arange(count, dtype=jnp.int32) * width)
    panel_sens = jnp.transpose(blocks, (1, 0, 2)).reshape(3, PANELS) * (1.0 / math.sqrt(PANELS * NF))
    vertex_sens = jnp.zeros((3, VERTS), jnp.float32)
    for corner in range(4):
        vertex_sens = vertex_sens.at[:, connect[corner]].add(0.25 * panel_sens)
    return (adjoint, vertex_sens, objective)
```

```python
import functools
import math

import jax
import jax.numpy as jnp
from jax import lax
from jax.experimental import pallas as pl
from jax.experimental.pallas import tpu as pltpu
from jax.sharding import PartitionSpec as P

SOFT = 1.0
LANES = 128
STEP = 16
MESH = pl.DeviceIdType.MESH
SIN_COEF = (6.283182818550509, -41.34142139863338, 81.59618387150631, -76.58010050947591, 41.205394790207706, -12.27126223106381)
COS_COEF = (0.999999221570582, -19.73898251610168, 64.92872660897218, -85.2723968955171, 58.7940381912709, -21.076781284621926)
MAGIC = 12582912.0


def horner(coefs, x):
    total = jnp.full_like(x, coefs[-1])
    for coef in coefs[-2::-1]:
        total = total * x + coef
    return total


def sincos_turns(turns):
    part = turns - ((turns + MAGIC) - MAGIC)
    square = part * part
    return part * horner(SIN_COEF, square), horner(COS_COEF, square)


def kernel(
    dims,
    cen_ref,
    str_ref,
    inv_ref,
    wave_ref,
    field_ref,
    targ_ref,
    lists_ref,
    conn_ref,
    adj_out,
    vert_out,
    obj_out,
    square_buf,
    src_buf,
    tgt_buf,
    src_rows,
    list_buf,
    list_rows,
    count_buf,
    green_cos,
    green_sin,
    eta_acc,
    eta_buf,
    resid_buf,
    send_source,
    recv_source,
    mu_src,
    mu_tgt,
    mu_rows,
    deriv_re,
    deriv_im,
    sens_buf,
    vert_send,
    vert_recv,
    send_row,
    recv_row,
    send_col,
    recv_col,
):
    rows, cols, own, freqs, points, listed, keep = dims
    sources, targets = rows * own, cols * own
    pos_at, inv_at = 2 * freqs, 2 * freqs + 8
    row, col = lax.axis_index("row"), lax.axis_index("col")

    def row_peer(k):
        return (lax.rem(row + k, rows), col)

    def col_peer(k):
        return (row, lax.rem(col + k, cols))

    barrier = pltpu.get_barrier_semaphore()
    for k in range(1, rows):
        pl.semaphore_signal(barrier, inc=1, device_id=row_peer(k), device_id_type=MESH)
    for k in range(1, cols):
        pl.semaphore_signal(barrier, inc=1, device_id=col_peer(k), device_id_type=MESH)

    own_src = pl.ds(pl.multiple_of(row * own, own), own)
    own_tgt = pl.ds(pl.multiple_of(col * own, own), own)

    square_buf[...] = jnp.zeros_like(square_buf)
    square_buf[0 : 2 * freqs, 0:own] = str_ref[...]
    square_buf[pos_at : pos_at + 3, 0:own] = cen_ref[...]
    square_buf[inv_at : inv_at + 2 * freqs, 0:own] = inv_ref[...]
    mine = jnp.transpose(square_buf[...])[0:own, :]
    src_buf[own_src, :] = mine
    tgt_buf[own_tgt, :] = mine

    def push(stage, source, target, peer, sems, k):
        copy = pltpu.make_async_remote_copy(
            src_ref=source,
            dst_ref=target,
            send_sem=sems[0].at[stage, k],
            recv_sem=sems[1].at[stage, k],
            device_id=peer,
            device_id_type=MESH,
        )
        copy.start()
        return copy

    row_sems, col_sems = (send_row, recv_row), (send_col, recv_col)
    pl.semaphore_wait(barrier, rows + cols - 2)
    done = []
    first = [
        push(0, src_buf.at[own_src], src_buf.at[own_src], row_peer(k), row_sems, k)
        for k in range(1, rows)
    ]
    side = [
        push(0, tgt_buf.at[own_tgt], tgt_buf.at[own_tgt], col_peer(k), col_sems, k)
        for k in range(1, cols)
    ]

    list_buf[...] = jnp.zeros_like(list_buf)
    list_buf[:, 0:listed] = lists_ref[...].astype(jnp.float32)
    list_rows[...] = jnp.transpose(list_buf[...])

    def count_step(block, carry):
        start = pl.multiple_of(block * own, own)
        ids = lax.broadcasted_iota(jnp.int32, (own, points), 0) + (block * cols + col) * own
        ids = ids.astype(jnp.float32)
        total = jnp.zeros((own, points), jnp.float32)
        for entry in range(listed):
            total = total + jnp.where(list_rows[entry : entry + 1, :] == ids, 1.0, 0.0)
        count_buf[pl.ds(start, own), :] = total
        return carry

    lax.fori_loop(0, rows, count_step, 0)
    eta_acc[...] = jnp.zeros_like(eta_acc)
    field = [field_ref[axis : axis + 1, :] for axis in range(3)]
    waves = [wave_ref[f] for f in range(freqs)]
    turns = [wave * (0.5 / math.pi) for wave in waves]

    for copy in first:
        copy.wait_recv()

    def field_step(step, carry):
        span = pl.ds(pl.multiple_of(step * STEP, STEP), STEP)
        block = src_buf[span, :]
        squared = SOFT
        for axis in range(3):
            gap = field[axis] - block[:, pos_at + axis : pos_at + axis + 1]
            squared = gap * gap + squared
        inverse = lax.rsqrt(squared)
        distance = squared * inverse
        gain = count_buf[span, :] * inverse
        for f in range(freqs):
            sine, cosine = sincos_turns(distance * turns[f])
            cosine, sine = cosine * gain, sine * gain
            green_cos[f, span, :] = cosine
            green_sin[f, span, :] = sine
            real, imag = block[:, f : f + 1], block[:, freqs + f : freqs + f + 1]
            part_real = cosine * real - sine * imag
            part_imag = cosine * imag + sine * real
            eta_acc[f] += jnp.sum(part_real.reshape(STEP // 8, 8, points), axis=0)
            eta_acc[freqs + f] += jnp.sum(part_imag.reshape(STEP // 8, 8, points), axis=0)
        return carry

    lax.fori_loop(0, sources // STEP, field_step, 0)
    eta_buf[col] = jnp.sum(eta_acc[...], axis=1)
    eta_copies = [
        push(1, eta_buf.at[col], eta_buf.at[col], col_peer(k), col_sems, k)
        for k in range(1, cols)
    ]

    for copy in side:
        copy.wait_recv()
    src_rows[...] = jnp.transpose(src_buf[...])
    place = [src_rows[pos_at + axis : pos_at + axis + 1, :] for axis in range(3)]

    def gaps(block):
        return [block[:, pos_at + axis : pos_at + axis + 1] - place[axis] for axis in range(3)]

    def lengths(offset):
        squared = offset[0] * offset[0] + offset[1] * offset[1] + offset[2] * offset[2] + SOFT
        inverse = lax.rsqrt(squared)
        return squared * inverse, inverse

    def derivative(f, distance, inverse_sq):
        phase = distance * waves[f]
        sine, cosine = sincos_turns(distance * turns[f])
        return -(cosine + phase * sine) * inverse_sq, (phase * cosine - sine) * inverse_sq

    if keep:

        def deriv_step(step, carry):
            span = pl.ds(pl.multiple_of(step * STEP, STEP), STEP)
            distance, inverse = lengths(gaps(tgt_buf[span, :]))
            for f in range(freqs):
                real, imag = derivative(f, distance, inverse * inverse)
                deriv_re[f, span, :] = real
                deriv_im[f, span, :] = imag
            return carry

        lax.fori_loop(0, targets // STEP, deriv_step, 0)

    for copy in eta_copies:
        copy.wait_recv()
    eta = eta_buf[0]
    for k in range(1, cols):
        eta = eta + eta_buf[k]
    resid = eta - targ_ref[...]
    resid_buf[...] = resid
    misfit = jnp.sum(jnp.sum(resid * resid, axis=0, keepdims=True), axis=1, keepdims=True)
    lane = lax.broadcasted_iota(jnp.int32, (STEP, LANES), 1)

    def source_step(step, carry):
        span = pl.ds(pl.multiple_of(step * STEP, STEP), STEP)
        total = jnp.where(lane == 2 * freqs, misfit, 0.0)
        for f in range(freqs):
            cosine, sine = green_cos[f, span, :], green_sin[f, span, :]
            real = resid_buf[f : f + 1, :]
            imag = resid_buf[freqs + f : freqs + f + 1, :]
            sum_real = jnp.sum(cosine * real + sine * imag, axis=1, keepdims=True)
            sum_imag = jnp.sum(cosine * imag - sine * real, axis=1, keepdims=True)
            total = jnp.where(lane == f, sum_real, total)
            total = jnp.where(lane == freqs + f, sum_imag, total)
        send_source[span, :] = total
        return carry

    lax.fori_loop(0, sources // STEP, source_step, 0)
    source_copies = []
    for k in range(1, rows):
        there = pl.ds(pl.multiple_of(lax.rem(row + k, rows) * own, own), own)
        source_copies.append(
            push(1, send_source.at[there], recv_source.at[own_src], row_peer(k), row_sems, k)
        )
    recv_source[own_src, :] = send_source[own_src, :]
    base = row * targets
    vertex = lax.broadcasted_iota(jnp.int32, (targets, targets), 0) + base
    share = jnp.zeros((targets, targets), jnp.float32)
    for corner in range(4):
        share = share + jnp.where(conn_ref[corner : corner + 1, :] == vertex, 0.25, 0.0)
    for copy in source_copies:
        copy.wait_recv()
    source = recv_source[0:own, :]
    for r in range(1, rows):
        source = source + recv_source[r * own : (r + 1) * own, :]
    objective = source[:, 2 * freqs : 2 * freqs + 1] / (freqs * points * rows) + 1e-06
    obj_out[...] = objective[0:1, :]
    source = source / objective
    lane = lax.broadcasted_iota(jnp.int32, (own, LANES), 1)
    low = lane < freqs
    inv_own = pltpu.roll(mine, LANES - inv_at, 1)
    inv_turn = jnp.where(low, -pltpu.roll(inv_own, LANES - freqs, 1), pltpu.roll(inv_own, freqs, 1))
    real = jnp.where(low, source, pltpu.roll(source, freqs, 1))
    imag = jnp.where(low, pltpu.roll(source, LANES - freqs, 1), source)
    mu = jnp.where(lane < 2 * freqs, real * inv_own + imag * inv_turn, 0.0)
    mu_src[own_src, :] = mu
    mu_tgt[own_tgt, :] = mu
    mu_copies = [
        push(2, mu_src.at[own_src], mu_src.at[own_src], row_peer(k), row_sems, k)
        for k in range(1, rows)
    ] + [
        push(2, mu_tgt.at[own_tgt], mu_tgt.at[own_tgt], col_peer(k), col_sems, k)
        for k in range(1, cols)
    ]
    square_buf[0:own, :] = mu
    adj_out[...] = jnp.transpose(square_buf[...])[0 : 2 * freqs, 0:own]
    for copy in mu_copies:
        copy.wait_recv()
    mu_rows[...] = jnp.transpose(mu_src[...])
    scale = 1.0 / math.sqrt(sources * cols * freqs)
    lane = lax.broadcasted_iota(jnp.int32, (STEP, LANES), 1)

    def sens_step(step, carry):
        span = pl.ds(pl.multiple_of(step * STEP, STEP), STEP)
        block, tmu = tgt_buf[span, :], mu_tgt[span, :]
        offset = gaps(block)
        distance, inverse = lengths(offset)
        weight = jnp.zeros((STEP, sources), jnp.float32)
        for f in range(freqs):
            g = freqs + f
            if keep:
                der_real, der_imag = deriv_re[f, span, :], deriv_im[f, span, :]
            else:
                der_real, der_imag = derivative(f, distance, inverse * inverse)
            t_real, t_imag = block[:, f : f + 1], block[:, g : g + 1]
            tm_real, tm_imag = tmu[:, f : f + 1], tmu[:, g : g + 1]
            s_real, s_imag = src_rows[f : f + 1, :], src_rows[g : g + 1, :]
            sm_real, sm_imag = mu_rows[f : f + 1, :], mu_rows[g : g + 1, :]
            prod_real = tm_real * s_real - tm_imag * s_imag + sm_real * t_real - sm_imag * t_imag
            prod_imag = tm_real * s_imag + tm_imag * s_real + sm_real * t_imag + sm_imag * t_real
            weight = weight + (prod_real * der_real - prod_imag * der_imag)
        weight = weight * inverse
        total = jnp.zeros((STEP, LANES), jnp.float32)
        for axis in range(3):
            part = jnp.sum(weight * offset[axis], axis=1, keepdims=True)
            total = jnp.where(lane == axis, part * scale, total)
        sens_buf[span, :] = total
        return carry

    lax.fori_loop(0, targets // STEP, sens_step, 0)
    vert_send[...] = jnp.dot(
        share,
        sens_buf[...],
        preferred_element_type=jnp.float32,
        precision=lax.Precision.HIGHEST,
    )
    vert_copies = []
    for k in range(1, cols):
        there = pl.ds(pl.multiple_of(lax.rem(col + k, cols) * own, own), own)
        vert_copies.append(
            push(3, vert_send.at[there], vert_recv.at[own_tgt], col_peer(k), col_sems, k)
        )
    vert_recv[own_tgt, :] = vert_send[own_tgt, :]
    for copy in vert_copies:
        copy.wait_recv()
    total = vert_recv[0:own, :]
    for k in range(1, cols):
        total = total + vert_recv[k * own : (k + 1) * own, :]
    square_buf[0:own, :] = total
    vert_out[...] = jnp.transpose(square_buf[...])[0:3, 0:own]
    for copy in first + side + eta_copies + source_copies + mu_copies + vert_copies:
        copy.wait_send()


def on_device(centroids, strengths, self_inv, wavenumbers, field_pos, targets, lists, connect):
    own = centroids.shape[1]
    rows, cols = lax.axis_size("row"), lax.axis_size("col")
    freqs = wavenumbers.shape[0]
    points, listed = lists.shape
    sources, block = rows * own, cols * own
    keep = freqs * block * sources * 8 <= 16 * 2**20
    kept = (freqs, block, sources) if keep else (1, 8, LANES)
    f32 = jnp.float32
    vmem = pl.BlockSpec(memory_space=pltpu.VMEM)
    smem = pl.BlockSpec(memory_space=pltpu.SMEM)
    adjoint, vertex, objective = pl.pallas_call(
        functools.partial(kernel, (rows, cols, own, freqs, points, listed, keep)),
        out_shape=(
            jax.ShapeDtypeStruct((2 * freqs, own), f32),
            jax.ShapeDtypeStruct((3, own), f32),
            jax.ShapeDtypeStruct((1, 1), f32),
        ),
        in_specs=[vmem, vmem, vmem, smem, vmem, vmem, vmem, vmem],
        out_specs=(vmem, vmem, vmem),
        scratch_shapes=[
            pltpu.VMEM((LANES, LANES), f32),
            pltpu.VMEM((sources, LANES), f32),
            pltpu.VMEM((block, LANES), f32),
            pltpu.VMEM((LANES, sources), f32),
            pltpu.VMEM((points, LANES), f32),
            pltpu.VMEM((LANES, points), f32),
            pltpu.VMEM((sources, points), f32),
            pltpu.VMEM((freqs, sources, points), f32),
            pltpu.VMEM((freqs, sources, points), f32),
            pltpu.VMEM((2 * freqs, 8, points), f32),
            pltpu.VMEM((cols, 2 * freqs, points), f32),
            pltpu.VMEM((2 * freqs, points), f32),
            pltpu.VMEM((sources, LANES), f32),
            pltpu.VMEM((sources, LANES), f32),
            pltpu.VMEM((sources, LANES), f32),
            pltpu.VMEM((block, LANES), f32),
            pltpu.VMEM((LANES, sources), f32),
            pltpu.VMEM(kept, f32),
            pltpu.VMEM(kept, f32),
            pltpu.VMEM((block, LANES), f32),
            pltpu.VMEM((block, LANES), f32),
            pltpu.VMEM((block, LANES), f32),
            pltpu.SemaphoreType.DMA((3, rows)),
            pltpu.SemaphoreType.DMA((3, rows)),
            pltpu.SemaphoreType.DMA((4, cols)),
            pltpu.SemaphoreType.DMA((4, cols)),
        ],
        compiler_params=pltpu.CompilerParams(
            collective_id=0, has_side_effects=True, vmem_limit_bytes=52 * 2**20
        ),
    )(centroids, strengths, self_inv, wavenumbers, field_pos, targets, lists, connect)
    return adjoint, vertex, objective.reshape(())


def solution(mesh):
    return jax.shard_map(
        on_device,
        mesh=mesh,
        in_specs=(
            P(None, ("row", "col")),
            P(None, ("row", "col")),
            P(None, ("row", "col")),
            P(),
            P(None, "row"),
            P(None, "row"),
            P("row", None),
            P(None, "row"),
        ),
        out_specs=(P(None, ("row", "col")), P(None, ("row", "col")), P()),
        check_vma=False,
    )
```

```python
import functools
import math

import jax
import jax.numpy as jnp
from jax import lax
from jax.experimental import pallas as pl
from jax.experimental.pallas import tpu as pltpu
from jax.sharding import PartitionSpec as P

SOFT = 1.0
LANES = 128
STEP = 16
MESH = pl.DeviceIdType.MESH
SIN_COEF = (6.283182818550509, -41.34142139863338, 81.59618387150631, -76.58010050947591, 41.205394790207706, -12.27126223106381)
COS_COEF = (0.999999221570582, -19.73898251610168, 64.92872660897218, -85.2723968955171, 58.7940381912709, -21.076781284621926)
MAGIC = 12582912.0


def horner(coefs, x):
    total = jnp.full_like(x, coefs[-1])
    for coef in coefs[-2::-1]:
        total = total * x + coef
    return total


def sincos_turns(turns):
    part = turns - ((turns + MAGIC) - MAGIC)
    square = part * part
    return part * horner(SIN_COEF, square), horner(COS_COEF, square)


def kernel(
    dims,
    cen_ref,
    str_ref,
    inv_ref,
    wave_ref,
    field_ref,
    targ_ref,
    lists_ref,
    conn_ref,
    adj_out,
    vert_out,
    obj_out,
    square_buf,
    src_pack,
    tgt_pack,
    src_buf,
    tgt_buf,
    src_rows,
    list_rows,
    count_buf,
    green_cos,
    green_sin,
    eta_acc,
    eta_buf,
    resid_buf,
    send_source,
    recv_source,
    mu_src_pack,
    mu_tgt_pack,
    mu_src,
    mu_tgt,
    mu_rows,
    deriv_re,
    deriv_im,
    turned_re,
    turned_im,
    sens_buf,
    vert_send,
    vert_recv,
    send_row,
    recv_row,
    send_col,
    recv_col,
):
    rows, cols, own, freqs, points, listed, keep = dims
    sources, targets = rows * own, cols * own
    pos_at, inv_at = 2 * freqs, 2 * freqs + 8
    row, col = lax.axis_index("row"), lax.axis_index("col")

    def row_peer(k):
        return (lax.rem(row + k, rows), col)

    def col_peer(k):
        return (row, lax.rem(col + k, cols))

    barrier = pltpu.get_barrier_semaphore()
    for k in range(1, rows):
        pl.semaphore_signal(barrier, inc=1, device_id=row_peer(k), device_id_type=MESH)
    for k in range(1, cols):
        pl.semaphore_signal(barrier, inc=1, device_id=col_peer(k), device_id_type=MESH)

    own_tgt = pl.ds(pl.multiple_of(col * own, own), own)
    groups = LANES // (2 * freqs)
    part = own // groups

    def slot(index, size, depth):
        return pl.ds(pl.multiple_of(index * depth, depth), size)

    def pack(block):
        total = block[0:part, :]
        for g in range(1, groups):
            total = total + pltpu.roll(block[g * part : (g + 1) * part, :], g * 2 * freqs, 1)
        return total

    def unpack(block, shift):
        parts = []
        for g in range(groups):
            by = (shift - g * 2 * freqs) % LANES
            parts.append(pltpu.roll(block, by, 1) if by else block)
        return jnp.concatenate(parts, axis=0)

    wide = lax.broadcasted_iota(jnp.int32, (own, LANES), 1)

    square_buf[...] = jnp.zeros_like(square_buf)
    square_buf[0 : 2 * freqs, 0:own] = str_ref[...]
    square_buf[pos_at : pos_at + 3, 0:own] = cen_ref[...]
    square_buf[inv_at : inv_at + 2 * freqs, 0:own] = inv_ref[...]
    mine = jnp.transpose(square_buf[...])[0:own, :]
    packed = jnp.concatenate(
        [
            pack(jnp.where(wide < pos_at, mine, 0.0)),
            pack(jnp.where(wide < 8, pltpu.roll(mine, LANES - pos_at, 1), 0.0)),
        ],
        axis=0,
    )
    src_mine, tgt_mine = slot(row, 2 * part, 2 * part), slot(col, 2 * part, 2 * part)
    src_pack[src_mine, :] = packed
    tgt_pack[tgt_mine, :] = packed

    def describe(stage, source, target, peer, sems, k):
        return pltpu.make_async_remote_copy(
            src_ref=source,
            dst_ref=target,
            send_sem=sems[0].at[stage, k],
            recv_sem=sems[1].at[stage, k],
            device_id=peer,
            device_id_type=MESH,
        )

    def push(*what):
        copy = describe(*what)
        copy.start()
        return copy

    row_sems, col_sems = (send_row, recv_row), (send_col, recv_col)
    pl.semaphore_wait(barrier, rows + cols - 2)
    first = [
        push(0, src_pack.at[src_mine], src_pack.at[src_mine], row_peer(k), row_sems, k)
        for k in range(1, rows)
    ]
    side = [
        push(0, tgt_pack.at[tgt_mine], tgt_pack.at[tgt_mine], col_peer(k), col_sems, k)
        for k in range(1, cols)
    ]

    list_rows[...] = lists_ref[...].astype(jnp.float32)

    def count_step(block, carry):
        start = pl.multiple_of(block * own, own)
        ids = lax.broadcasted_iota(jnp.int32, (own, points), 0) + (block * cols + col) * own
        ids = ids.astype(jnp.float32)
        total = jnp.zeros((own, points), jnp.float32)
        for entry in range(listed):
            total = total + jnp.where(list_rows[entry : entry + 1, :] == ids, 1.0, 0.0)
        count_buf[pl.ds(start, own), :] = total
        return carry

    lax.fori_loop(0, rows, count_step, 0)
    eta_acc[...] = jnp.zeros_like(eta_acc)
    field = [field_ref[axis : axis + 1, :] for axis in range(3)]
    waves = [wave_ref[f] for f in range(freqs)]
    turns = [wave * (0.5 / math.pi) for wave in waves]

    def open_pack(packs, opened):
        def open_step(block, carry):
            both = packs[slot(block, 2 * part, 2 * part), :]
            strength, place = unpack(both[0:part, :], 0), unpack(both[part:, :], pos_at)
            opened[slot(block, own, own), :] = jnp.where(wide < pos_at, strength, place)
            return carry

        return open_step

    for copy in first:
        copy.wait_recv()
    lax.fori_loop(0, rows, open_pack(src_pack, src_buf), 0)

    def field_step(step, carry):
        span = pl.ds(pl.multiple_of(step * STEP, STEP), STEP)
        block = src_buf[span, :]
        squared = SOFT
        for axis in range(3):
            gap = field[axis] - block[:, pos_at + axis : pos_at + axis + 1]
            squared = gap * gap + squared
        inverse = lax.rsqrt(squared)
        distance = squared * inverse
        gain = count_buf[span, :] * inverse
        for f in range(freqs):
            sine, cosine = sincos_turns(distance * turns[f])
            cosine, sine = cosine * gain, sine * gain
            green_cos[f, span, :] = cosine
            green_sin[f, span, :] = sine
            real, imag = block[:, f : f + 1], block[:, freqs + f : freqs + f + 1]
            part_real = cosine * real - sine * imag
            part_imag = cosine * imag + sine * real
            eta_acc[f] += jnp.sum(part_real.reshape(STEP // 8, 8, points), axis=0)
            eta_acc[freqs + f] += jnp.sum(part_imag.reshape(STEP // 8, 8, points), axis=0)
        return carry

    lax.fori_loop(0, sources // STEP, field_step, 0)
    eta_buf[col] = jnp.sum(eta_acc[...], axis=1)
    eta_copies = [
        push(1, eta_buf.at[col], eta_buf.at[col], col_peer(k), col_sems, k)
        for k in range(1, cols)
    ]

    for copy in side:
        copy.wait_recv()
    lax.fori_loop(0, cols, open_pack(tgt_pack, tgt_buf), 0)
    src_rows[...] = jnp.transpose(src_buf[...])
    place = [src_rows[pos_at + axis : pos_at + axis + 1, :] for axis in range(3)]

    def gaps(block):
        return [block[:, pos_at + axis : pos_at + axis + 1] - place[axis] for axis in range(3)]

    def lengths(offset):
        squared = offset[0] * offset[0] + offset[1] * offset[1] + offset[2] * offset[2] + SOFT
        inverse = lax.rsqrt(squared)
        return squared * inverse, inverse

    def derivative(f, distance, inverse):
        inverse_cube = inverse * inverse * inverse
        phase = distance * waves[f]
        sine, cosine = sincos_turns(distance * turns[f])
        return -(cosine + phase * sine) * inverse_cube, (phase * cosine - sine) * inverse_cube

    if keep:

        def deriv_step(step, carry):
            span = pl.ds(pl.multiple_of(step * STEP, STEP), STEP)
            distance, inverse = lengths(gaps(tgt_buf[span, :]))
            for f in range(freqs):
                real, imag = derivative(f, distance, inverse)
                deriv_re[f, span, :] = real
                deriv_im[f, span, :] = imag
            return carry

        lax.fori_loop(0, targets // STEP, deriv_step, 0)

    for copy in eta_copies:
        copy.wait_recv()
    eta = eta_buf[0]
    for k in range(1, cols):
        eta = eta + eta_buf[k]
    resid = eta - targ_ref[...]
    resid_buf[...] = resid
    misfit = jnp.sum(jnp.sum(resid * resid, axis=0, keepdims=True), axis=1, keepdims=True)
    lane = lax.broadcasted_iota(jnp.int32, (STEP, LANES), 1)

    def source_sums(start):
        span = pl.ds(pl.multiple_of(start, STEP), STEP)
        total = jnp.zeros((STEP, LANES), jnp.float32)
        for f in range(freqs):
            cosine, sine = green_cos[f, span, :], green_sin[f, span, :]
            real = resid_buf[f : f + 1, :]
            imag = resid_buf[freqs + f : freqs + f + 1, :]
            sum_real = jnp.sum(cosine * real + sine * imag, axis=1, keepdims=True)
            sum_imag = jnp.sum(cosine * imag - sine * real, axis=1, keepdims=True)
            total = jnp.where(lane == f, sum_real, total)
            total = jnp.where(lane == freqs + f, sum_imag, total)
        return total

    def source_block(r):
        sums = [source_sums(r * own + step) for step in range(0, own, STEP)]
        return pack(jnp.concatenate(sums, axis=0))

    misfit_rows = jnp.broadcast_to(misfit, (part, LANES))

    def source_copy(k):
        there = slot(lax.rem(row + k, rows), 2 * part, 2 * part)
        return describe(
            1, send_source.at[there], recv_source.at[src_mine], row_peer(k), row_sems, k
        )

    def source_step(k, carry):
        r = lax.rem(row + k, rows)
        send_source[slot(r, 2 * part, 2 * part), :] = jnp.concatenate(
            [source_block(r), misfit_rows], axis=0
        )
        source_copy(k).start()
        return carry

    lax.fori_loop(1, rows, source_step, 0)
    recv_source[src_mine, :] = jnp.concatenate([source_block(row), misfit_rows], axis=0)
    if keep:

        def turn_step(step, carry):
            span = pl.ds(pl.multiple_of(step * STEP, STEP), STEP)
            block = tgt_buf[span, :]
            for f in range(freqs):
                g = freqs + f
                real, imag = deriv_re[f, span, :], deriv_im[f, span, :]
                t_real, t_imag = block[:, f : f + 1], block[:, g : g + 1]
                s_real, s_imag = src_rows[f : f + 1, :], src_rows[g : g + 1, :]
                turned_re[f, span, :] = t_real * real - t_imag * imag
                turned_im[f, span, :] = t_real * imag + t_imag * real
                deriv_re[f, span, :] = s_real * real - s_imag * imag
                deriv_im[f, span, :] = s_real * imag + s_imag * real
            return carry

        lax.fori_loop(0, targets // STEP, turn_step, 0)
    base = row * targets
    vertex = lax.broadcasted_iota(jnp.int32, (targets, targets), 0) + base
    share = jnp.zeros((targets, targets), jnp.float32)
    for corner in range(4):
        share = share + jnp.where(conn_ref[corner : corner + 1, :] == vertex, 0.25, 0.0)
    for k in range(1, rows):
        source_copy(k).wait_recv()
    both = recv_source[0 : 2 * part, :]
    for r in range(1, rows):
        both = both + recv_source[r * 2 * part : (r + 1) * 2 * part, :]
    objective = both[part : part + 1, 0:1] / (freqs * points * rows) + 1e-06
    obj_out[...] = objective
    source = unpack(both[0:part, :] / objective, 0)
    low = wide < freqs
    inv_own = pltpu.roll(mine, LANES - inv_at, 1)
    inv_turn = jnp.where(low, -pltpu.roll(inv_own, LANES - freqs, 1), pltpu.roll(inv_own, freqs, 1))
    real = jnp.where(low, source, pltpu.roll(source, freqs, 1))
    imag = jnp.where(low, pltpu.roll(source, LANES - freqs, 1), source)
    mu = jnp.where(wide < 2 * freqs, real * inv_own + imag * inv_turn, 0.0)
    packed = pack(mu)
    src_mine, tgt_mine = slot(row, part, part), slot(col, part, part)
    mu_src_pack[src_mine, :] = packed
    mu_tgt_pack[tgt_mine, :] = packed
    mu_copies = [
        push(2, mu_src_pack.at[src_mine], mu_src_pack.at[src_mine], row_peer(k), row_sems, k)
        for k in range(1, rows)
    ] + [
        push(2, mu_tgt_pack.at[tgt_mine], mu_tgt_pack.at[tgt_mine], col_peer(k), col_sems, k)
        for k in range(1, cols)
    ]
    square_buf[0:own, :] = mu
    adj_out[...] = jnp.transpose(square_buf[...])[0 : 2 * freqs, 0:own]
    for copy in mu_copies:
        copy.wait_recv()

    def open_mu(packs, opened):
        def open_step(block, carry):
            opened[slot(block, own, own), :] = unpack(packs[slot(block, part, part), :], 0)
            return carry

        return open_step

    lax.fori_loop(0, rows, open_mu(mu_src_pack, mu_src), 0)
    lax.fori_loop(0, cols, open_mu(mu_tgt_pack, mu_tgt), 0)
    mu_rows[...] = jnp.transpose(mu_src[...])
    scale = 1.0 / math.sqrt(sources * cols * freqs)
    lane = lax.broadcasted_iota(jnp.int32, (STEP, LANES), 1)

    def sens_step(step, carry):
        span = pl.ds(pl.multiple_of(step * STEP, STEP), STEP)
        block, tmu = tgt_buf[span, :], mu_tgt[span, :]
        offset = gaps(block)
        distance, inverse = lengths(offset)
        weight = jnp.zeros((STEP, sources), jnp.float32)
        for f in range(freqs):
            g = freqs + f
            tm_real, tm_imag = tmu[:, f : f + 1], tmu[:, g : g + 1]
            sm_real, sm_imag = mu_rows[f : f + 1, :], mu_rows[g : g + 1, :]
            if keep:
                weight = weight + (tm_real * deriv_re[f, span, :] - tm_imag * deriv_im[f, span, :])
                weight = weight + (sm_real * turned_re[f, span, :] - sm_imag * turned_im[f, span, :])
                continue
            der_real, der_imag = derivative(f, distance, inverse)
            t_real, t_imag = block[:, f : f + 1], block[:, g : g + 1]
            s_real, s_imag = src_rows[f : f + 1, :], src_rows[g : g + 1, :]
            prod_real = tm_real * s_real - tm_imag * s_imag + sm_real * t_real - sm_imag * t_imag
            prod_imag = tm_real * s_imag + tm_imag * s_real + sm_real * t_imag + sm_imag * t_real
            weight = weight + (prod_real * der_real - prod_imag * der_imag)
        total = jnp.zeros((STEP, LANES), jnp.float32)
        for axis in range(3):
            part = jnp.sum(weight * offset[axis], axis=1, keepdims=True)
            total = jnp.where(lane == axis, part * scale, total)
        sens_buf[span, :] = total
        return carry

    lax.fori_loop(0, targets // STEP, sens_step, 0)
    vert_send[...] = jnp.dot(
        share,
        sens_buf[...],
        preferred_element_type=jnp.float32,
        precision=lax.Precision.HIGHEST,
    )
    vert_copies = []
    for k in range(1, cols):
        there = pl.ds(pl.multiple_of(lax.rem(col + k, cols) * own, own), own)
        vert_copies.append(
            push(3, vert_send.at[there], vert_recv.at[own_tgt], col_peer(k), col_sems, k)
        )
    vert_recv[own_tgt, :] = vert_send[own_tgt, :]
    for copy in vert_copies:
        copy.wait_recv()
    total = vert_recv[0:own, :]
    for k in range(1, cols):
        total = total + vert_recv[k * own : (k + 1) * own, :]
    square_buf[0:own, :] = total
    vert_out[...] = jnp.transpose(square_buf[...])[0:3, 0:own]
    for copy in first + side + eta_copies + mu_copies + vert_copies:
        copy.wait_send()
    for k in range(1, rows):
        source_copy(k).wait_send()


def on_device(centroids, strengths, self_inv, wavenumbers, field_pos, targets, lists, connect):
    own = centroids.shape[1]
    rows, cols = lax.axis_size("row"), lax.axis_size("col")
    freqs = wavenumbers.shape[0]
    points, listed = lists.shape
    pack_rows = 2 * own * 2 * freqs // LANES
    sources, block = rows * own, cols * own
    keep = freqs * block * sources * 8 <= 16 * 2**20
    kept = (freqs, block, sources) if keep else (1, 8, LANES)
    f32 = jnp.float32
    vmem = pl.BlockSpec(memory_space=pltpu.VMEM)
    smem = pl.BlockSpec(memory_space=pltpu.SMEM)
    adjoint, vertex, objective = pl.pallas_call(
        functools.partial(kernel, (rows, cols, own, freqs, points, listed, keep)),
        out_shape=(
            jax.ShapeDtypeStruct((2 * freqs, own), f32),
            jax.ShapeDtypeStruct((3, own), f32),
            jax.ShapeDtypeStruct((1, 1), f32),
        ),
        in_specs=[vmem, vmem, vmem, smem, vmem, vmem, vmem, vmem],
        out_specs=(vmem, vmem, vmem),
        scratch_shapes=[
            pltpu.VMEM((LANES, LANES), f32),
            pltpu.VMEM((rows * pack_rows, LANES), f32),
            pltpu.VMEM((cols * pack_rows, LANES), f32),
            pltpu.VMEM((sources, LANES), f32),
            pltpu.VMEM((block, LANES), f32),
            pltpu.VMEM((LANES, sources), f32),
            pltpu.VMEM((listed, points), f32),
            pltpu.VMEM((sources, points), f32),
            pltpu.VMEM((freqs, sources, points), f32),
            pltpu.VMEM((freqs, sources, points), f32),
            pltpu.VMEM((2 * freqs, 8, points), f32),
            pltpu.VMEM((cols, 2 * freqs, points), f32),
            pltpu.VMEM((2 * freqs, points), f32),
            pltpu.VMEM((rows * pack_rows, LANES), f32),
            pltpu.VMEM((rows * pack_rows, LANES), f32),
            pltpu.VMEM((rows * pack_rows // 2, LANES), f32),
            pltpu.VMEM((cols * pack_rows // 2, LANES), f32),
            pltpu.VMEM((sources, LANES), f32),
            pltpu.VMEM((block, LANES), f32),
            pltpu.VMEM((LANES, sources), f32),
            pltpu.VMEM(kept, f32),
            pltpu.VMEM(kept, f32),
            pltpu.VMEM(kept, f32),
            pltpu.VMEM(kept, f32),
            pltpu.VMEM((block, LANES), f32),
            pltpu.VMEM((block, LANES), f32),
            pltpu.VMEM((block, LANES), f32),
            pltpu.SemaphoreType.DMA((3, rows)),
            pltpu.SemaphoreType.DMA((3, rows)),
            pltpu.SemaphoreType.DMA((4, cols)),
            pltpu.SemaphoreType.DMA((4, cols)),
        ],
        compiler_params=pltpu.CompilerParams(
            collective_id=0, has_side_effects=True, vmem_limit_bytes=52 * 2**20
        ),
    )(centroids, strengths, self_inv, wavenumbers, field_pos, targets, lists.T, connect)
    return adjoint, vertex, objective.reshape(())


def solution(mesh):
    return jax.shard_map(
        on_device,
        mesh=mesh,
        in_specs=(
            P(None, ("row", "col")),
            P(None, ("row", "col")),
            P(None, ("row", "col")),
            P(),
            P(None, "row"),
            P(None, "row"),
            P("row", None),
            P(None, "row"),
        ),
        out_specs=(P(None, ("row", "col")), P(None, ("row", "col")), P()),
        check_vma=False,
    )
```

```python
import functools
import math

import jax
import jax.numpy as jnp
from jax import lax
from jax.experimental import pallas as pl
from jax.experimental.pallas import tpu as pltpu
from jax.sharding import PartitionSpec as P

SOFT = 1.0
LANES = 128
STEP = 16
MESH = pl.DeviceIdType.MESH
SIN_COEF = (6.283182818550509, -41.34142139863338, 81.59618387150631, -76.58010050947591, 41.205394790207706, -12.27126223106381)
COS_COEF = (0.999999221570582, -19.73898251610168, 64.92872660897218, -85.2723968955171, 58.7940381912709, -21.076781284621926)
MAGIC = 12582912.0


def horner(coefs, x):
    total = jnp.full_like(x, coefs[-1])
    for coef in coefs[-2::-1]:
        total = total * x + coef
    return total


def sincos_turns(turns):
    part = turns - ((turns + MAGIC) - MAGIC)
    square = part * part
    return part * horner(SIN_COEF, square), horner(COS_COEF, square)


def kernel(
    dims,
    cen_hbm,
    str_hbm,
    inv_hbm,
    wave_ref,
    field_hbm,
    targ_hbm,
    lists_hbm,
    conn_hbm,
    adj_out,
    vert_out,
    obj_out,
    square_buf,
    src_pack,
    tgt_pack,
    src_buf,
    tgt_buf,
    src_rows,
    list_rows,
    count_buf,
    green_cos,
    green_sin,
    eta_acc,
    eta_buf,
    resid_buf,
    send_source,
    recv_source,
    mu_src_pack,
    mu_tgt_pack,
    mu_src,
    mu_tgt,
    mu_rows,
    deriv_re,
    deriv_im,
    turned_re,
    turned_im,
    sens_buf,
    vert_send,
    vert_recv,
    send_row,
    recv_row,
    send_col,
    recv_col,
    cen_ref,
    str_ref,
    inv_ref,
    field_ref,
    targ_ref,
    lists_ref,
    conn_ref,
    load_sem,
):
    rows, cols, own, freqs, points, listed, keep = dims
    sources, targets = rows * own, cols * own
    pos_at, inv_at = 2 * freqs, 2 * freqs + 8
    row, col = lax.axis_index("row"), lax.axis_index("col")

    loads = [
        pltpu.make_async_copy(there, here, load_sem.at[index])
        for index, (there, here) in enumerate(
            [
                (cen_hbm, cen_ref),
                (str_hbm, str_ref),
                (inv_hbm, inv_ref),
                (lists_hbm, lists_ref),
                (field_hbm, field_ref),
                (targ_hbm, targ_ref),
                (conn_hbm, conn_ref),
            ]
        )
    ]
    for load in loads:
        load.start()

    def row_peer(k):
        return (lax.rem(row + k, rows), col)

    def col_peer(k):
        return (row, lax.rem(col + k, cols))

    barrier = pltpu.get_barrier_semaphore()
    for k in range(1, rows):
        pl.semaphore_signal(barrier, inc=1, device_id=row_peer(k), device_id_type=MESH)
    for k in range(1, cols):
        pl.semaphore_signal(barrier, inc=1, device_id=col_peer(k), device_id_type=MESH)

    own_tgt = pl.ds(pl.multiple_of(col * own, own), own)
    groups = LANES // (2 * freqs)
    part = own // groups

    def slot(index, size, depth):
        return pl.ds(pl.multiple_of(index * depth, depth), size)

    def pack(block):
        total = block[0:part, :]
        for g in range(1, groups):
            total = total + pltpu.roll(block[g * part : (g + 1) * part, :], g * 2 * freqs, 1)
        return total

    def unpack(block, shift):
        parts = []
        for g in range(groups):
            by = (shift - g * 2 * freqs) % LANES
            parts.append(pltpu.roll(block, by, 1) if by else block)
        return jnp.concatenate(parts, axis=0)

    wide = lax.broadcasted_iota(jnp.int32, (own, LANES), 1)

    square_buf[...] = jnp.zeros_like(square_buf)
    for load in loads[:3]:
        load.wait()
    square_buf[0 : 2 * freqs, 0:own] = str_ref[...]
    square_buf[pos_at : pos_at + 3, 0:own] = cen_ref[...]
    square_buf[inv_at : inv_at + 2 * freqs, 0:own] = inv_ref[...]
    mine = jnp.transpose(square_buf[...])[0:own, :]
    packed = jnp.concatenate(
        [
            pack(jnp.where(wide < pos_at, mine, 0.0)),
            pack(jnp.where(wide < 8, pltpu.roll(mine, LANES - pos_at, 1), 0.0)),
        ],
        axis=0,
    )
    src_mine, tgt_mine = slot(row, 2 * part, 2 * part), slot(col, 2 * part, 2 * part)
    src_pack[src_mine, :] = packed
    tgt_pack[tgt_mine, :] = packed

    def describe(stage, source, target, peer, sems, k):
        return pltpu.make_async_remote_copy(
            src_ref=source,
            dst_ref=target,
            send_sem=sems[0].at[stage, k],
            recv_sem=sems[1].at[stage, k],
            device_id=peer,
            device_id_type=MESH,
        )

    def push(*what):
        copy = describe(*what)
        copy.start()
        return copy

    row_sems, col_sems = (send_row, recv_row), (send_col, recv_col)
    pl.semaphore_wait(barrier, rows + cols - 2)
    first = [
        push(0, src_pack.at[src_mine], src_pack.at[src_mine], row_peer(k), row_sems, k)
        for k in range(1, rows)
    ]
    side = [
        push(0, tgt_pack.at[tgt_mine], tgt_pack.at[tgt_mine], col_peer(k), col_sems, k)
        for k in range(1, cols)
    ]

    for load in loads[3:]:
        load.wait()
    list_rows[...] = lists_ref[...].astype(jnp.float32)

    def count_step(block, carry):
        start = pl.multiple_of(block * own, own)
        ids = lax.broadcasted_iota(jnp.int32, (own, points), 0) + (block * cols + col) * own
        ids = ids.astype(jnp.float32)
        total = jnp.zeros((own, points), jnp.float32)
        for entry in range(listed):
            total = total + jnp.where(list_rows[entry : entry + 1, :] == ids, 1.0, 0.0)
        count_buf[pl.ds(start, own), :] = total
        return carry

    lax.fori_loop(0, rows, count_step, 0)
    eta_acc[...] = jnp.zeros_like(eta_acc)
    field = [field_ref[axis : axis + 1, :] for axis in range(3)]
    waves = [wave_ref[f] for f in range(freqs)]
    turns = [wave * (0.5 / math.pi) for wave in waves]

    def open_pack(packs, opened):
        def open_step(block, carry):
            both = packs[slot(block, 2 * part, 2 * part), :]
            strength, place = unpack(both[0:part, :], 0), unpack(both[part:, :], pos_at)
            opened[slot(block, own, own), :] = jnp.where(wide < pos_at, strength, place)
            return carry

        return open_step

    for copy in first:
        copy.wait_recv()
    lax.fori_loop(0, rows, open_pack(src_pack, src_buf), 0)

    def field_step(step, carry):
        span = pl.ds(pl.multiple_of(step * STEP, STEP), STEP)
        block = src_buf[span, :]
        squared = SOFT
        for axis in range(3):
            gap = field[axis] - block[:, pos_at + axis : pos_at + axis + 1]
            squared = gap * gap + squared
        inverse = lax.rsqrt(squared)
        distance = squared * inverse
        gain = count_buf[span, :] * inverse
        for f in range(freqs):
            sine, cosine = sincos_turns(distance * turns[f])
            cosine, sine = cosine * gain, sine * gain
            green_cos[f, span, :] = cosine
            green_sin[f, span, :] = sine
            real, imag = block[:, f : f + 1], block[:, freqs + f : freqs + f + 1]
            part_real = cosine * real - sine * imag
            part_imag = cosine * imag + sine * real
            eta_acc[f] += jnp.sum(part_real.reshape(STEP // 8, 8, points), axis=0)
            eta_acc[freqs + f] += jnp.sum(part_imag.reshape(STEP // 8, 8, points), axis=0)
        return carry

    lax.fori_loop(0, sources // STEP, field_step, 0)
    eta_buf[col] = jnp.sum(eta_acc[...], axis=1)
    eta_copies = [
        push(1, eta_buf.at[col], eta_buf.at[col], col_peer(k), col_sems, k)
        for k in range(1, cols)
    ]

    for copy in side:
        copy.wait_recv()
    lax.fori_loop(0, cols, open_pack(tgt_pack, tgt_buf), 0)
    src_rows[...] = jnp.transpose(src_buf[...])
    place = [src_rows[pos_at + axis : pos_at + axis + 1, :] for axis in range(3)]

    def gaps(block):
        return [block[:, pos_at + axis : pos_at + axis + 1] - place[axis] for axis in range(3)]

    def lengths(offset):
        squared = offset[0] * offset[0] + offset[1] * offset[1] + offset[2] * offset[2] + SOFT
        inverse = lax.rsqrt(squared)
        return squared * inverse, inverse

    def derivative(f, distance, inverse):
        inverse_cube = inverse * inverse * inverse
        phase = distance * waves[f]
        sine, cosine = sincos_turns(distance * turns[f])
        return -(cosine + phase * sine) * inverse_cube, (phase * cosine - sine) * inverse_cube

    if keep:

        def deriv_step(step, carry):
            span = pl.ds(pl.multiple_of(step * STEP, STEP), STEP)
            distance, inverse = lengths(gaps(tgt_buf[span, :]))
            for f in range(freqs):
                real, imag = derivative(f, distance, inverse)
                deriv_re[f, span, :] = real
                deriv_im[f, span, :] = imag
            return carry

        lax.fori_loop(0, targets // STEP, deriv_step, 0)

    for copy in eta_copies:
        copy.wait_recv()
    eta = eta_buf[0]
    for k in range(1, cols):
        eta = eta + eta_buf[k]
    resid = eta - targ_ref[...]
    resid_buf[...] = resid
    misfit = jnp.sum(jnp.sum(resid * resid, axis=0, keepdims=True), axis=1, keepdims=True)
    lane = lax.broadcasted_iota(jnp.int32, (STEP, LANES), 1)

    def source_sums(start):
        span = pl.ds(pl.multiple_of(start, STEP), STEP)
        total = jnp.zeros((STEP, LANES), jnp.float32)
        for f in range(freqs):
            cosine, sine = green_cos[f, span, :], green_sin[f, span, :]
            real = resid_buf[f : f + 1, :]
            imag = resid_buf[freqs + f : freqs + f + 1, :]
            sum_real = jnp.sum(cosine * real + sine * imag, axis=1, keepdims=True)
            sum_imag = jnp.sum(cosine * imag - sine * real, axis=1, keepdims=True)
            total = jnp.where(lane == f, sum_real, total)
            total = jnp.where(lane == freqs + f, sum_imag, total)
        return total

    def source_block(r):
        sums = [source_sums(r * own + step) for step in range(0, own, STEP)]
        return pack(jnp.concatenate(sums, axis=0))

    misfit_rows = jnp.broadcast_to(misfit, (part, LANES))

    def source_copy(k):
        there = slot(lax.rem(row + k, rows), 2 * part, 2 * part)
        return describe(
            1, send_source.at[there], recv_source.at[src_mine], row_peer(k), row_sems, k
        )

    def source_step(k, carry):
        r = lax.rem(row + k, rows)
        send_source[slot(r, 2 * part, 2 * part), :] = jnp.concatenate(
            [source_block(r), misfit_rows], axis=0
        )
        source_copy(k).start()
        return carry

    lax.fori_loop(1, rows, source_step, 0)
    recv_source[src_mine, :] = jnp.concatenate([source_block(row), misfit_rows], axis=0)
    if keep:

        def turn_step(step, carry):
            span = pl.ds(pl.multiple_of(step * STEP, STEP), STEP)
            block = tgt_buf[span, :]
            for f in range(freqs):
                g = freqs + f
                real, imag = deriv_re[f, span, :], deriv_im[f, span, :]
                t_real, t_imag = block[:, f : f + 1], block[:, g : g + 1]
                s_real, s_imag = src_rows[f : f + 1, :], src_rows[g : g + 1, :]
                turned_re[f, span, :] = t_real * real - t_imag * imag
                turned_im[f, span, :] = t_real * imag + t_imag * real
                deriv_re[f, span, :] = s_real * real - s_imag * imag
                deriv_im[f, span, :] = s_real * imag + s_imag * real
            return carry

        lax.fori_loop(0, targets // STEP, turn_step, 0)
    base = row * targets
    vertex = lax.broadcasted_iota(jnp.int32, (targets, targets), 0) + base
    share = jnp.zeros((targets, targets), jnp.float32)
    for corner in range(4):
        share = share + jnp.where(conn_ref[corner : corner + 1, :] == vertex, 0.25, 0.0)
    for k in range(1, rows):
        source_copy(k).wait_recv()
    both = recv_source[0 : 2 * part, :]
    for r in range(1, rows):
        both = both + recv_source[r * 2 * part : (r + 1) * 2 * part, :]
    objective = both[part : part + 1, 0:1] / (freqs * points * rows) + 1e-06
    obj_out[...] = objective
    source = unpack(both[0:part, :] / objective, 0)
    low = wide < freqs
    inv_own = pltpu.roll(mine, LANES - inv_at, 1)
    inv_turn = jnp.where(low, -pltpu.roll(inv_own, LANES - freqs, 1), pltpu.roll(inv_own, freqs, 1))
    real = jnp.where(low, source, pltpu.roll(source, freqs, 1))
    imag = jnp.where(low, pltpu.roll(source, LANES - freqs, 1), source)
    mu = jnp.where(wide < 2 * freqs, real * inv_own + imag * inv_turn, 0.0)
    packed = pack(mu)
    src_mine, tgt_mine = slot(row, part, part), slot(col, part, part)
    mu_src_pack[src_mine, :] = packed
    mu_tgt_pack[tgt_mine, :] = packed
    mu_copies = [
        push(2, mu_src_pack.at[src_mine], mu_src_pack.at[src_mine], row_peer(k), row_sems, k)
        for k in range(1, rows)
    ] + [
        push(2, mu_tgt_pack.at[tgt_mine], mu_tgt_pack.at[tgt_mine], col_peer(k), col_sems, k)
        for k in range(1, cols)
    ]
    square_buf[0:own, :] = mu
    adj_out[...] = jnp.transpose(square_buf[...])[0 : 2 * freqs, 0:own]
    for copy in mu_copies:
        copy.wait_recv()

    def open_mu(packs, opened):
        def open_step(block, carry):
            opened[slot(block, own, own), :] = unpack(packs[slot(block, part, part), :], 0)
            return carry

        return open_step

    lax.fori_loop(0, rows, open_mu(mu_src_pack, mu_src), 0)
    lax.fori_loop(0, cols, open_mu(mu_tgt_pack, mu_tgt), 0)
    mu_rows[...] = jnp.transpose(mu_src[...])
    scale = 1.0 / math.sqrt(sources * cols * freqs)
    lane = lax.broadcasted_iota(jnp.int32, (STEP, LANES), 1)

    def sens_step(step, carry):
        span = pl.ds(pl.multiple_of(step * STEP, STEP), STEP)
        block, tmu = tgt_buf[span, :], mu_tgt[span, :]
        offset = gaps(block)
        distance, inverse = lengths(offset)
        weight = jnp.zeros((STEP, sources), jnp.float32)
        for f in range(freqs):
            g = freqs + f
            tm_real, tm_imag = tmu[:, f : f + 1], tmu[:, g : g + 1]
            sm_real, sm_imag = mu_rows[f : f + 1, :], mu_rows[g : g + 1, :]
            if keep:
                weight = weight + (tm_real * deriv_re[f, span, :] - tm_imag * deriv_im[f, span, :])
                weight = weight + (sm_real * turned_re[f, span, :] - sm_imag * turned_im[f, span, :])
                continue
            der_real, der_imag = derivative(f, distance, inverse)
            t_real, t_imag = block[:, f : f + 1], block[:, g : g + 1]
            s_real, s_imag = src_rows[f : f + 1, :], src_rows[g : g + 1, :]
            prod_real = tm_real * s_real - tm_imag * s_imag + sm_real * t_real - sm_imag * t_imag
            prod_imag = tm_real * s_imag + tm_imag * s_real + sm_real * t_imag + sm_imag * t_real
            weight = weight + (prod_real * der_real - prod_imag * der_imag)
        total = jnp.zeros((STEP, LANES), jnp.float32)
        for axis in range(3):
            part = jnp.sum(weight * offset[axis], axis=1, keepdims=True)
            total = jnp.where(lane == axis, part * scale, total)
        sens_buf[span, :] = total
        return carry

    lax.fori_loop(0, targets // STEP, sens_step, 0)
    vert_send[...] = jnp.dot(
        share,
        sens_buf[...],
        preferred_element_type=jnp.float32,
        precision=lax.Precision.HIGHEST,
    )
    vert_copies = []
    for k in range(1, cols):
        there = pl.ds(pl.multiple_of(lax.rem(col + k, cols) * own, own), own)
        vert_copies.append(
            push(3, vert_send.at[there], vert_recv.at[own_tgt], col_peer(k), col_sems, k)
        )
    vert_recv[own_tgt, :] = vert_send[own_tgt, :]
    for copy in vert_copies:
        copy.wait_recv()
    total = vert_recv[0:own, :]
    for k in range(1, cols):
        total = total + vert_recv[k * own : (k + 1) * own, :]
    square_buf[0:own, :] = total
    vert_out[...] = jnp.transpose(square_buf[...])[0:3, 0:own]
    for copy in first + side + eta_copies + mu_copies + vert_copies:
        copy.wait_send()
    for k in range(1, rows):
        source_copy(k).wait_send()


def on_device(centroids, strengths, self_inv, wavenumbers, field_pos, targets, lists, connect):
    own = centroids.shape[1]
    rows, cols = lax.axis_size("row"), lax.axis_size("col")
    freqs = wavenumbers.shape[0]
    points, listed = lists.shape
    pack_rows = 2 * own * 2 * freqs // LANES
    sources, block = rows * own, cols * own
    keep = freqs * block * sources * 8 <= 16 * 2**20
    kept = (freqs, block, sources) if keep else (1, 8, LANES)
    f32 = jnp.float32
    vmem = pl.BlockSpec(memory_space=pltpu.VMEM)
    hbm = pl.BlockSpec(memory_space=pltpu.HBM)
    smem = pl.BlockSpec(memory_space=pltpu.SMEM)
    adjoint, vertex, objective = pl.pallas_call(
        functools.partial(kernel, (rows, cols, own, freqs, points, listed, keep)),
        out_shape=(
            jax.ShapeDtypeStruct((2 * freqs, own), f32),
            jax.ShapeDtypeStruct((3, own), f32),
            jax.ShapeDtypeStruct((1, 1), f32),
        ),
        in_specs=[hbm, hbm, hbm, smem, hbm, hbm, hbm, hbm],
        out_specs=(vmem, vmem, vmem),
        scratch_shapes=[
            pltpu.VMEM((LANES, LANES), f32),
            pltpu.VMEM((rows * pack_rows, LANES), f32),
            pltpu.VMEM((cols * pack_rows, LANES), f32),
            pltpu.VMEM((sources, LANES), f32),
            pltpu.VMEM((block, LANES), f32),
            pltpu.VMEM((LANES, sources), f32),
            pltpu.VMEM((listed, points), f32),
            pltpu.VMEM((sources, points), f32),
            pltpu.VMEM((freqs, sources, points), f32),
            pltpu.VMEM((freqs, sources, points), f32),
            pltpu.VMEM((2 * freqs, 8, points), f32),
            pltpu.VMEM((cols, 2 * freqs, points), f32),
            pltpu.VMEM((2 * freqs, points), f32),
            pltpu.VMEM((rows * pack_rows, LANES), f32),
            pltpu.VMEM((rows * pack_rows, LANES), f32),
            pltpu.VMEM((rows * pack_rows // 2, LANES), f32),
            pltpu.VMEM((cols * pack_rows // 2, LANES), f32),
            pltpu.VMEM((sources, LANES), f32),
            pltpu.VMEM((block, LANES), f32),
            pltpu.VMEM((LANES, sources), f32),
            pltpu.VMEM(kept, f32),
            pltpu.VMEM(kept, f32),
            pltpu.VMEM(kept, f32),
            pltpu.VMEM(kept, f32),
            pltpu.VMEM((block, LANES), f32),
            pltpu.VMEM((block, LANES), f32),
            pltpu.VMEM((block, LANES), f32),
            pltpu.SemaphoreType.DMA((3, rows)),
            pltpu.SemaphoreType.DMA((3, rows)),
            pltpu.SemaphoreType.DMA((4, cols)),
            pltpu.SemaphoreType.DMA((4, cols)),
            pltpu.VMEM(centroids.shape, f32),
            pltpu.VMEM(strengths.shape, f32),
            pltpu.VMEM(self_inv.shape, f32),
            pltpu.VMEM(field_pos.shape, f32),
            pltpu.VMEM(targets.shape, f32),
            pltpu.VMEM((listed, points), jnp.int32),
            pltpu.VMEM(connect.shape, jnp.int32),
            pltpu.SemaphoreType.DMA((7,)),
        ],
        compiler_params=pltpu.CompilerParams(
            collective_id=0, has_side_effects=True, vmem_limit_bytes=60 * 2**20
        ),
    )(centroids, strengths, self_inv, wavenumbers, field_pos, targets, lists.T, connect)
    return adjoint, vertex, objective.reshape(())


def solution(mesh):
    return jax.shard_map(
        on_device,
        mesh=mesh,
        in_specs=(
            P(None, ("row", "col")),
            P(None, ("row", "col")),
            P(None, ("row", "col")),
            P(),
            P(None, "row"),
            P(None, "row"),
            P("row", None),
            P(None, "row"),
        ),
        out_specs=(P(None, ("row", "col")), P(None, ("row", "col")), P()),
        check_vma=False,
    )
```

```python
import functools
import math

import jax
import jax.numpy as jnp
from jax import lax
from jax.experimental import pallas as pl
from jax.experimental.pallas import tpu as pltpu
from jax.sharding import PartitionSpec as P

SOFT = 1.0
LANES = 128
STEP = 16
UNROLL = 4
MESH = pl.DeviceIdType.MESH
SIN_COEF = (6.283182818550509, -41.34142139863338, 81.59618387150631, -76.58010050947591, 41.205394790207706, -12.27126223106381)
COS_COEF = (0.999999221570582, -19.73898251610168, 64.92872660897218, -85.2723968955171, 58.7940381912709, -21.076781284621926)
MAGIC = 12582912.0


def horner(coefs, x):
    total = jnp.full_like(x, coefs[-1])
    for coef in coefs[-2::-1]:
        total = total * x + coef
    return total


def sincos_turns(turns):
    part = turns - ((turns + MAGIC) - MAGIC)
    square = part * part
    return part * horner(SIN_COEF, square), horner(COS_COEF, square)


def kernel(
    dims,
    cen_hbm,
    str_hbm,
    inv_hbm,
    wave_ref,
    field_hbm,
    targ_hbm,
    lists_hbm,
    conn_hbm,
    adj_out,
    vert_out,
    obj_out,
    square_buf,
    src_pack,
    tgt_pack,
    src_buf,
    tgt_buf,
    src_rows,
    list_rows,
    field_rows,
    onehot,
    pieces,
    green_cos,
    green_sin,
    eta_buf,
    source_rows,
    send_source,
    recv_source,
    mu_src_pack,
    mu_tgt_pack,
    mu_src,
    mu_tgt,
    mu_rows,
    deriv_re,
    deriv_im,
    turned_re,
    turned_im,
    sens_buf,
    vert_send,
    vert_recv,
    send_row,
    recv_row,
    send_col,
    recv_col,
    cen_ref,
    str_ref,
    inv_ref,
    field_ref,
    targ_ref,
    lists_ref,
    conn_ref,
    load_sem,
):
    rows, cols, own, freqs, points, listed, keep = dims
    sources, targets = rows * own, cols * own
    pos_at, inv_at = 2 * freqs, 2 * freqs + 8
    row, col = lax.axis_index("row"), lax.axis_index("col")

    loads = [
        pltpu.make_async_copy(there, here, load_sem.at[index])
        for index, (there, here) in enumerate(
            [
                (cen_hbm, cen_ref),
                (str_hbm, str_ref),
                (inv_hbm, inv_ref),
                (lists_hbm, lists_ref),
                (field_hbm, field_ref),
                (targ_hbm, targ_ref),
                (conn_hbm, conn_ref),
            ]
        )
    ]
    for load in loads:
        load.start()

    def row_peer(k):
        return (lax.rem(row + k, rows), col)

    def col_peer(k):
        return (row, lax.rem(col + k, cols))

    barrier = pltpu.get_barrier_semaphore()
    for k in range(1, rows):
        pl.semaphore_signal(barrier, inc=1, device_id=row_peer(k), device_id_type=MESH)
    for k in range(1, cols):
        pl.semaphore_signal(barrier, inc=1, device_id=col_peer(k), device_id_type=MESH)

    own_tgt = pl.ds(pl.multiple_of(col * own, own), own)
    groups = LANES // (2 * freqs)
    part = own // groups

    def slot(index, size, depth):
        return pl.ds(pl.multiple_of(index * depth, depth), size)

    def pack(block):
        total = block[0:part, :]
        for g in range(1, groups):
            total = total + pltpu.roll(block[g * part : (g + 1) * part, :], g * 2 * freqs, 1)
        return total

    def unpack(block, shift):
        parts = []
        for g in range(groups):
            by = (shift - g * 2 * freqs) % LANES
            parts.append(pltpu.roll(block, by, 1) if by else block)
        return jnp.concatenate(parts, axis=0)

    wide = lax.broadcasted_iota(jnp.int32, (own, LANES), 1)

    square_buf[...] = jnp.zeros_like(square_buf)
    for load in loads[:3]:
        load.wait()
    square_buf[0 : 2 * freqs, 0:own] = str_ref[...]
    square_buf[pos_at : pos_at + 3, 0:own] = cen_ref[...]
    square_buf[inv_at : inv_at + 2 * freqs, 0:own] = inv_ref[...]
    mine = jnp.transpose(square_buf[...])[0:own, :]
    packed = jnp.concatenate(
        [
            pack(jnp.where(wide < pos_at, mine, 0.0)),
            pack(jnp.where(wide < 8, pltpu.roll(mine, LANES - pos_at, 1), 0.0)),
        ],
        axis=0,
    )
    src_mine, tgt_mine = slot(row, 2 * part, 2 * part), slot(col, 2 * part, 2 * part)
    src_pack[src_mine, :] = packed
    tgt_pack[tgt_mine, :] = packed

    def describe(stage, source, target, peer, sems, k):
        return pltpu.make_async_remote_copy(
            src_ref=source,
            dst_ref=target,
            send_sem=sems[0].at[stage, k],
            recv_sem=sems[1].at[stage, k],
            device_id=peer,
            device_id_type=MESH,
        )

    def push(*what):
        copy = describe(*what)
        copy.start()
        return copy

    row_sems, col_sems = (send_row, recv_row), (send_col, recv_col)
    pl.semaphore_wait(barrier, rows + cols - 2)
    first = [
        push(0, src_pack.at[src_mine], src_pack.at[src_mine], row_peer(k), row_sems, k)
        for k in range(1, rows)
    ]
    side = [
        push(0, tgt_pack.at[tgt_mine], tgt_pack.at[tgt_mine], col_peer(k), col_sems, k)
        for k in range(1, cols)
    ]

    for load in loads[3:]:
        load.wait()
    ids = lists_ref[...].astype(jnp.float32)
    owner = jnp.floor((ids + 0.5) * (1.0 / own))
    turn = jnp.floor((owner + 0.5) * (1.0 / cols))
    place = ids - owner * own + turn * own
    list_rows[...] = jnp.where(owner - turn * cols == col.astype(jnp.float32), place, -1.0)
    field_rows[...] = jnp.zeros_like(field_rows)
    field_rows[0:3, :] = field_ref[...]

    def onehot_step(entry, carry):
        places = list_rows[pl.ds(entry, 1), :]
        for start in range(0, sources, own):
            ids = lax.broadcasted_iota(jnp.int32, (own, points), 0) + start
            hit = jnp.where(places == ids.astype(jnp.float32), 1.0, 0.0)
            onehot[entry, start : start + own, :] = hit.astype(jnp.bfloat16)
        return carry

    lax.fori_loop(0, listed, onehot_step, 0)
    waves = [wave_ref[f] for f in range(freqs)]
    turns = [wave * (0.5 / math.pi) for wave in waves]
    sub = lax.broadcasted_iota(jnp.int32, (freqs, points), 0)
    turn_col = jnp.zeros((freqs, points), jnp.float32)
    for f in range(freqs):
        turn_col = jnp.where(sub == f, turns[f], turn_col)

    def open_pack(packs, opened):
        def open_step(block, carry):
            both = packs[slot(block, 2 * part, 2 * part), :]
            strength, place = unpack(both[0:part, :], 0), unpack(both[part:, :], pos_at)
            opened[slot(block, own, own), :] = jnp.where(wide < pos_at, strength, place)
            return carry

        return open_step

    for copy in first:
        copy.wait_recv()
    lax.fori_loop(0, rows, open_pack(src_pack, src_buf), 0)
    src_rows[...] = jnp.transpose(src_buf[...])
    tall = pos_at + 8

    def split(value, count):
        parts = []
        for _ in range(count):
            part = value.astype(jnp.bfloat16)
            parts.append(part)
            value = value - part.astype(jnp.float32)
        return parts

    extent = lax.broadcasted_iota(jnp.int32, (tall, sources), 0)
    values = jnp.where(extent < pos_at + 3, src_rows[0:tall, :], 0.0)
    parts = [part.astype(jnp.float32) for part in split(values, 3)]
    parts = [part[0:pos_at] for part in parts] + [part[pos_at:] for part in parts]
    spare = jnp.zeros((pieces.shape[0] - 3 * tall, sources), jnp.float32)
    pieces[...] = jnp.concatenate(parts + [spare], axis=0).astype(jnp.bfloat16)

    def field_step(step, carry):
        eta_real, eta_imag = carry
        for unrolled in range(UNROLL):
            entry = step * UNROLL + unrolled
            near = jnp.dot(pieces[...], onehot[entry], preferred_element_type=jnp.float32)
            strength = near[0:pos_at] + near[pos_at : 2 * pos_at] + near[2 * pos_at : 3 * pos_at]
            where = near[3 * pos_at :]
            where = where[0:8] + where[8:16] + where[16:24]
            gap = field_rows[...] - where
            squared = jnp.sum(gap * gap, axis=0, keepdims=True) + SOFT
            inverse = lax.rsqrt(squared)
            sine, cosine = sincos_turns(turn_col * (squared * inverse))
            cosine, sine = cosine * inverse, sine * inverse
            green_cos[entry] = cosine
            green_sin[entry] = sine
            real, imag = strength[0:freqs], strength[freqs:]
            eta_real = eta_real + (cosine * real - sine * imag)
            eta_imag = eta_imag + (cosine * imag + sine * real)
        return eta_real, eta_imag

    zero = jnp.zeros((freqs, points), jnp.float32)
    eta_real, eta_imag = lax.fori_loop(0, listed // UNROLL, field_step, (zero, zero))
    eta_buf[col] = jnp.concatenate([eta_real, eta_imag], axis=0)
    eta_copies = [
        push(1, eta_buf.at[col], eta_buf.at[col], col_peer(k), col_sems, k)
        for k in range(1, cols)
    ]

    for copy in side:
        copy.wait_recv()
    lax.fori_loop(0, cols, open_pack(tgt_pack, tgt_buf), 0)
    place = [src_rows[pos_at + axis : pos_at + axis + 1, :] for axis in range(3)]

    def gaps(block):
        return [block[:, pos_at + axis : pos_at + axis + 1] - place[axis] for axis in range(3)]

    def lengths(offset):
        squared = offset[0] * offset[0] + offset[1] * offset[1] + offset[2] * offset[2] + SOFT
        inverse = lax.rsqrt(squared)
        return squared * inverse, inverse

    def derivative(f, distance, inverse):
        inverse_cube = inverse * inverse * inverse
        phase = distance * waves[f]
        sine, cosine = sincos_turns(distance * turns[f])
        return -(cosine + phase * sine) * inverse_cube, (phase * cosine - sine) * inverse_cube

    if keep:

        def deriv_step(step, carry):
            span = pl.ds(pl.multiple_of(step * STEP, STEP), STEP)
            distance, inverse = lengths(gaps(tgt_buf[span, :]))
            for f in range(freqs):
                real, imag = derivative(f, distance, inverse)
                deriv_re[f, span, :] = real
                deriv_im[f, span, :] = imag
            return carry

        lax.fori_loop(0, targets // STEP, deriv_step, 0)

    for copy in eta_copies:
        copy.wait_recv()
    eta = eta_buf[0]
    for k in range(1, cols):
        eta = eta + eta_buf[k]
    resid = eta - targ_ref[...]
    misfit = jnp.sum(jnp.sum(resid * resid, axis=0, keepdims=True), axis=1, keepdims=True)

    res_real, res_imag = resid[0:freqs], resid[freqs:]

    def scatter_step(step, total):
        for unrolled in range(UNROLL):
            entry = step * UNROLL + unrolled
            cosine, sine = green_cos[entry], green_sin[entry]
            real = cosine * res_real + sine * res_imag
            imag = cosine * res_imag - sine * res_real
            terms = jnp.concatenate(split(jnp.concatenate([real, imag], axis=0), 2), axis=0)
            total = total + lax.dot_general(
                terms,
                onehot[entry],
                (((1,), (1,)), ((), ())),
                preferred_element_type=jnp.float32,
            )
        return total

    total = jnp.zeros((4 * freqs, sources), jnp.float32)
    total = lax.fori_loop(0, listed // UNROLL, scatter_step, total)
    source_rows[...] = jnp.zeros_like(source_rows)
    source_rows[0 : 2 * freqs, :] = total[0 : 2 * freqs] + total[2 * freqs :]
    src_buf[...] = jnp.transpose(source_rows[...])

    def source_block(r):
        return pack(src_buf[slot(r, own, own), :])

    misfit_rows = jnp.broadcast_to(misfit, (part, LANES))

    def source_copy(k):
        there = slot(lax.rem(row + k, rows), 2 * part, 2 * part)
        return describe(
            1, send_source.at[there], recv_source.at[src_mine], row_peer(k), row_sems, k
        )

    def source_step(k, carry):
        r = lax.rem(row + k, rows)
        send_source[slot(r, 2 * part, 2 * part), :] = jnp.concatenate(
            [source_block(r), misfit_rows], axis=0
        )
        source_copy(k).start()
        return carry

    lax.fori_loop(1, rows, source_step, 0)
    recv_source[src_mine, :] = jnp.concatenate([source_block(row), misfit_rows], axis=0)
    if keep:

        def turn_step(step, carry):
            span = pl.ds(pl.multiple_of(step * STEP, STEP), STEP)
            block = tgt_buf[span, :]
            for f in range(freqs):
                g = freqs + f
                real, imag = deriv_re[f, span, :], deriv_im[f, span, :]
                t_real, t_imag = block[:, f : f + 1], block[:, g : g + 1]
                s_real, s_imag = src_rows[f : f + 1, :], src_rows[g : g + 1, :]
                turned_re[f, span, :] = t_real * real - t_imag * imag
                turned_im[f, span, :] = t_real * imag + t_imag * real
                deriv_re[f, span, :] = s_real * real - s_imag * imag
                deriv_im[f, span, :] = s_real * imag + s_imag * real
            return carry

        lax.fori_loop(0, targets // STEP, turn_step, 0)
    base = row * targets
    vertex = lax.broadcasted_iota(jnp.int32, (targets, targets), 0) + base
    share = jnp.zeros((targets, targets), jnp.float32)
    for corner in range(4):
        share = share + jnp.where(conn_ref[corner : corner + 1, :] == vertex, 0.25, 0.0)
    for k in range(1, rows):
        source_copy(k).wait_recv()
    both = recv_source[0 : 2 * part, :]
    for r in range(1, rows):
        both = both + recv_source[r * 2 * part : (r + 1) * 2 * part, :]
    objective = both[part : part + 1, 0:1] / (freqs * points * rows) + 1e-06
    obj_out[...] = objective
    source = unpack(both[0:part, :] / objective, 0)
    low = wide < freqs
    inv_own = pltpu.roll(mine, LANES - inv_at, 1)
    inv_turn = jnp.where(low, -pltpu.roll(inv_own, LANES - freqs, 1), pltpu.roll(inv_own, freqs, 1))
    real = jnp.where(low, source, pltpu.roll(source, freqs, 1))
    imag = jnp.where(low, pltpu.roll(source, LANES - freqs, 1), source)
    mu = jnp.where(wide < 2 * freqs, real * inv_own + imag * inv_turn, 0.0)
    packed = pack(mu)
    src_mine, tgt_mine = slot(row, part, part), slot(col, part, part)
    mu_src_pack[src_mine, :] = packed
    mu_tgt_pack[tgt_mine, :] = packed
    mu_copies = [
        push(2, mu_src_pack.at[src_mine], mu_src_pack.at[src_mine], row_peer(k), row_sems, k)
        for k in range(1, rows)
    ] + [
        push(2, mu_tgt_pack.at[tgt_mine], mu_tgt_pack.at[tgt_mine], col_peer(k), col_sems, k)
        for k in range(1, cols)
    ]
    square_buf[0:own, :] = mu
    adj_out[...] = jnp.transpose(square_buf[...])[0 : 2 * freqs, 0:own]
    for copy in mu_copies:
        copy.wait_recv()

    def open_mu(packs, opened):
        def open_step(block, carry):
            opened[slot(block, own, own), :] = unpack(packs[slot(block, part, part), :], 0)
            return carry

        return open_step

    lax.fori_loop(0, rows, open_mu(mu_src_pack, mu_src), 0)
    lax.fori_loop(0, cols, open_mu(mu_tgt_pack, mu_tgt), 0)
    mu_rows[...] = jnp.transpose(mu_src[...])
    scale = 1.0 / math.sqrt(sources * cols * freqs)
    lane = lax.broadcasted_iota(jnp.int32, (STEP, LANES), 1)

    def sens_step(step, carry):
        span = pl.ds(pl.multiple_of(step * STEP, STEP), STEP)
        block, tmu = tgt_buf[span, :], mu_tgt[span, :]
        offset = gaps(block)
        distance, inverse = lengths(offset)
        weight = jnp.zeros((STEP, sources), jnp.float32)
        for f in range(freqs):
            g = freqs + f
            tm_real, tm_imag = tmu[:, f : f + 1], tmu[:, g : g + 1]
            sm_real, sm_imag = mu_rows[f : f + 1, :], mu_rows[g : g + 1, :]
            if keep:
                weight = weight + (tm_real * deriv_re[f, span, :] - tm_imag * deriv_im[f, span, :])
                weight = weight + (sm_real * turned_re[f, span, :] - sm_imag * turned_im[f, span, :])
                continue
            der_real, der_imag = derivative(f, distance, inverse)
            t_real, t_imag = block[:, f : f + 1], block[:, g : g + 1]
            s_real, s_imag = src_rows[f : f + 1, :], src_rows[g : g + 1, :]
            prod_real = tm_real * s_real - tm_imag * s_imag + sm_real * t_real - sm_imag * t_imag
            prod_imag = tm_real * s_imag + tm_imag * s_real + sm_real * t_imag + sm_imag * t_real
            weight = weight + (prod_real * der_real - prod_imag * der_imag)
        total = jnp.zeros((STEP, LANES), jnp.float32)
        for axis in range(3):
            part = jnp.sum(weight * offset[axis], axis=1, keepdims=True)
            total = jnp.where(lane == axis, part * scale, total)
        sens_buf[span, :] = total
        return carry

    lax.fori_loop(0, targets // STEP, sens_step, 0)
    vert_send[...] = jnp.dot(
        share,
        sens_buf[...],
        preferred_element_type=jnp.float32,
        precision=lax.Precision.HIGHEST,
    )
    vert_copies = []
    for k in range(1, cols):
        there = pl.ds(pl.multiple_of(lax.rem(col + k, cols) * own, own), own)
        vert_copies.append(
            push(3, vert_send.at[there], vert_recv.at[own_tgt], col_peer(k), col_sems, k)
        )
    vert_recv[own_tgt, :] = vert_send[own_tgt, :]
    for copy in vert_copies:
        copy.wait_recv()
    total = vert_recv[0:own, :]
    for k in range(1, cols):
        total = total + vert_recv[k * own : (k + 1) * own, :]
    square_buf[0:own, :] = total
    vert_out[...] = jnp.transpose(square_buf[...])[0:3, 0:own]
    for copy in first + side + eta_copies + mu_copies + vert_copies:
        copy.wait_send()
    for k in range(1, rows):
        source_copy(k).wait_send()


def on_device(centroids, strengths, self_inv, wavenumbers, field_pos, targets, lists, connect):
    own = centroids.shape[1]
    rows, cols = lax.axis_size("row"), lax.axis_size("col")
    freqs = wavenumbers.shape[0]
    points, listed = lists.shape
    pack_rows = 2 * own * 2 * freqs // LANES
    sources, block = rows * own, cols * own
    keep = freqs * block * sources * 8 <= 16 * 2**20
    kept = (freqs, block, sources) if keep else (1, 8, LANES)
    f32 = jnp.float32
    vmem = pl.BlockSpec(memory_space=pltpu.VMEM)
    hbm = pl.BlockSpec(memory_space=pltpu.HBM)
    smem = pl.BlockSpec(memory_space=pltpu.SMEM)
    adjoint, vertex, objective = pl.pallas_call(
        functools.partial(kernel, (rows, cols, own, freqs, points, listed, keep)),
        out_shape=(
            jax.ShapeDtypeStruct((2 * freqs, own), f32),
            jax.ShapeDtypeStruct((3, own), f32),
            jax.ShapeDtypeStruct((1, 1), f32),
        ),
        in_specs=[hbm, hbm, hbm, smem, hbm, hbm, hbm, hbm],
        out_specs=(vmem, vmem, vmem),
        scratch_shapes=[
            pltpu.VMEM((LANES, LANES), f32),
            pltpu.VMEM((rows * pack_rows, LANES), f32),
            pltpu.VMEM((cols * pack_rows, LANES), f32),
            pltpu.VMEM((sources, LANES), f32),
            pltpu.VMEM((block, LANES), f32),
            pltpu.VMEM((LANES, sources), f32),
            pltpu.VMEM((listed, points), f32),
            pltpu.VMEM((8, points), f32),
            pltpu.VMEM((listed, sources, points), jnp.bfloat16),
            pltpu.VMEM((-(-3 * (2 * freqs + 8) // 16) * 16, sources), jnp.bfloat16),
            pltpu.VMEM((listed, freqs, points), f32),
            pltpu.VMEM((listed, freqs, points), f32),
            pltpu.VMEM((cols, 2 * freqs, points), f32),
            pltpu.VMEM((LANES, sources), f32),
            pltpu.VMEM((rows * pack_rows, LANES), f32),
            pltpu.VMEM((rows * pack_rows, LANES), f32),
            pltpu.VMEM((rows * pack_rows // 2, LANES), f32),
            pltpu.VMEM((cols * pack_rows // 2, LANES), f32),
            pltpu.VMEM((sources, LANES), f32),
            pltpu.VMEM((block, LANES), f32),
            pltpu.VMEM((LANES, sources), f32),
            pltpu.VMEM(kept, f32),
            pltpu.VMEM(kept, f32),
            pltpu.VMEM(kept, f32),
            pltpu.VMEM(kept, f32),
            pltpu.VMEM((block, LANES), f32),
            pltpu.VMEM((block, LANES), f32),
            pltpu.VMEM((block, LANES), f32),
            pltpu.SemaphoreType.DMA((3, rows)),
            pltpu.SemaphoreType.DMA((3, rows)),
            pltpu.SemaphoreType.DMA((4, cols)),
            pltpu.SemaphoreType.DMA((4, cols)),
            pltpu.VMEM(centroids.shape, f32),
            pltpu.VMEM(strengths.shape, f32),
            pltpu.VMEM(self_inv.shape, f32),
            pltpu.VMEM(field_pos.shape, f32),
            pltpu.VMEM(targets.shape, f32),
            pltpu.VMEM((listed, points), jnp.int32),
            pltpu.VMEM(connect.shape, jnp.int32),
            pltpu.SemaphoreType.DMA((7,)),
        ],
        compiler_params=pltpu.CompilerParams(
            collective_id=0, has_side_effects=True, vmem_limit_bytes=60 * 2**20
        ),
    )(centroids, strengths, self_inv, wavenumbers, field_pos, targets, lists.T, connect)
    return adjoint, vertex, objective.reshape(())


def solution(mesh):
    return jax.shard_map(
        on_device,
        mesh=mesh,
        in_specs=(
            P(None, ("row", "col")),
            P(None, ("row", "col")),
            P(None, ("row", "col")),
            P(),
            P(None, "row"),
            P(None, "row"),
            P("row", None),
            P(None, "row"),
        ),
        out_specs=(P(None, ("row", "col")), P(None, ("row", "col")), P()),
        check_vma=False,
    )
```

```python
import functools
import math

import jax
import jax.numpy as jnp
from jax import lax
from jax.experimental import pallas as pl
from jax.experimental.pallas import tpu as pltpu
from jax.sharding import PartitionSpec as P

SOFT = 1.0
LANES = 128
STEP = 16
MESH = pl.DeviceIdType.MESH
SIN_COEF = (6.283182818550509, -41.34142139863338, 81.59618387150631, -76.58010050947591, 41.205394790207706, -12.27126223106381)
COS_COEF = (0.999999221570582, -19.73898251610168, 64.92872660897218, -85.2723968955171, 58.7940381912709, -21.076781284621926)
MAGIC = 12582912.0


def horner(coefs, x):
    total = jnp.full_like(x, coefs[-1])
    for coef in coefs[-2::-1]:
        total = total * x + coef
    return total


def sincos_turns(turns):
    part = turns - ((turns + MAGIC) - MAGIC)
    square = part * part
    return part * horner(SIN_COEF, square), horner(COS_COEF, square)


def kernel(
    dims,
    cen_hbm,
    str_hbm,
    inv_hbm,
    wave_ref,
    field_hbm,
    targ_hbm,
    lists_hbm,
    conn_hbm,
    adj_out,
    vert_out,
    obj_out,
    square_buf,
    src_pack,
    tgt_pack,
    src_buf,
    tgt_buf,
    src_rows,
    list_rows,
    count_buf,
    green_cos,
    green_sin,
    eta_acc,
    eta_buf,
    resid_buf,
    send_source,
    recv_source,
    mu_src_pack,
    mu_tgt_pack,
    mu_src,
    mu_tgt,
    mu_rows,
    deriv_re,
    deriv_im,
    turned_re,
    turned_im,
    sens_buf,
    vert_send,
    vert_recv,
    send_row,
    recv_row,
    send_col,
    recv_col,
    cen_ref,
    str_ref,
    inv_ref,
    field_ref,
    targ_ref,
    lists_ref,
    conn_ref,
    load_sem,
):
    rows, cols, own, freqs, points, listed, keep = dims
    sources, targets = rows * own, cols * own
    pos_at, inv_at = 2 * freqs, 2 * freqs + 8
    row, col = lax.axis_index("row"), lax.axis_index("col")

    loads = [
        pltpu.make_async_copy(there, here, load_sem.at[index])
        for index, (there, here) in enumerate(
            [
                (cen_hbm, cen_ref),
                (str_hbm, str_ref),
                (inv_hbm, inv_ref),
                (lists_hbm, lists_ref),
                (field_hbm, field_ref),
                (targ_hbm, targ_ref),
                (conn_hbm, conn_ref),
            ]
        )
    ]
    for load in loads:
        load.start()

    if rows & (rows - 1):
        raise ValueError("rows")

    def row_mate(k):
        mate, bit = 0, 1
        while bit < rows:
            mate = mate + bit * lax.rem(lax.div(row, bit) + lax.div(k, bit), 2)
            bit *= 2
        return mate

    def row_peer(k):
        return (row_mate(jnp.int32(k)), col)

    def col_peer(k):
        return (row, lax.rem(col + k, cols))

    barrier = pltpu.get_barrier_semaphore()
    for k in range(1, rows):
        pl.semaphore_signal(barrier, inc=1, device_id=row_peer(k), device_id_type=MESH)
    for k in range(1, cols):
        pl.semaphore_signal(barrier, inc=1, device_id=col_peer(k), device_id_type=MESH)

    own_tgt = pl.ds(pl.multiple_of(col * own, own), own)
    groups = LANES // (2 * freqs)
    part = own // groups

    def slot(index, size, depth):
        return pl.ds(pl.multiple_of(index * depth, depth), size)

    def pack(block):
        total = block[0:part, :]
        for g in range(1, groups):
            total = total + pltpu.roll(block[g * part : (g + 1) * part, :], g * 2 * freqs, 1)
        return total

    def unpack(block, shift):
        parts = []
        for g in range(groups):
            by = (shift - g * 2 * freqs) % LANES
            parts.append(pltpu.roll(block, by, 1) if by else block)
        return jnp.concatenate(parts, axis=0)

    wide = lax.broadcasted_iota(jnp.int32, (own, LANES), 1)

    square_buf[...] = jnp.zeros_like(square_buf)
    for load in loads[:3]:
        load.wait()
    square_buf[0 : 2 * freqs, 0:own] = str_ref[...]
    square_buf[pos_at : pos_at + 3, 0:own] = cen_ref[...]
    square_buf[inv_at : inv_at + 2 * freqs, 0:own] = inv_ref[...]
    mine = jnp.transpose(square_buf[...])[0:own, :]
    packed = jnp.concatenate(
        [
            pack(jnp.where(wide < pos_at, mine, 0.0)),
            pack(jnp.where(wide < 8, pltpu.roll(mine, LANES - pos_at, 1), 0.0)),
        ],
        axis=0,
    )
    src_mine, tgt_mine = slot(row, 2 * part, 2 * part), slot(col, 2 * part, 2 * part)
    src_pack[src_mine, :] = packed
    tgt_pack[tgt_mine, :] = packed

    def describe(stage, source, target, peer, sems, k):
        return pltpu.make_async_remote_copy(
            src_ref=source,
            dst_ref=target,
            send_sem=sems[0].at[stage, k],
            recv_sem=sems[1].at[stage, k],
            device_id=peer,
            device_id_type=MESH,
        )

    def push(*what):
        copy = describe(*what)
        copy.start()
        return copy

    row_sems, col_sems = (send_row, recv_row), (send_col, recv_col)
    pl.semaphore_wait(barrier, rows + cols - 2)

    def panel_copy(k):
        return describe(
            0, src_pack.at[src_mine], src_pack.at[src_mine], row_peer(k), row_sems, k
        )

    for k in range(rows - 1, 0, -1):
        panel_copy(k).start()
    side = [
        push(0, tgt_pack.at[tgt_mine], tgt_pack.at[tgt_mine], col_peer(k), col_sems, k)
        for k in range(1, cols)
    ]

    for load in loads[3:]:
        load.wait()
    list_rows[...] = lists_ref[...].astype(jnp.float32)

    def count_step(block, carry):
        start = pl.multiple_of(block * own, own)
        ids = lax.broadcasted_iota(jnp.int32, (own, points), 0) + (block * cols + col) * own
        ids = ids.astype(jnp.float32)
        total = jnp.zeros((own, points), jnp.float32)
        for entry in range(listed):
            total = total + jnp.where(list_rows[entry : entry + 1, :] == ids, 1.0, 0.0)
        count_buf[pl.ds(start, own), :] = total
        return carry

    lax.fori_loop(0, rows, count_step, 0)
    eta_acc[...] = jnp.zeros_like(eta_acc)
    field = [field_ref[axis : axis + 1, :] for axis in range(3)]
    waves = [wave_ref[f] for f in range(freqs)]
    turns = [wave * (0.5 / math.pi) for wave in waves]

    def open_pack(packs, opened):
        def open_step(block, carry):
            both = packs[slot(block, 2 * part, 2 * part), :]
            strength, place = unpack(both[0:part, :], 0), unpack(both[part:, :], pos_at)
            opened[slot(block, own, own), :] = jnp.where(wide < pos_at, strength, place)
            return carry

        return open_step


    def field_step(start):
        span = pl.ds(pl.multiple_of(start, STEP), STEP)
        block = src_buf[span, :]
        squared = SOFT
        for axis in range(3):
            gap = field[axis] - block[:, pos_at + axis : pos_at + axis + 1]
            squared = gap * gap + squared
        inverse = lax.rsqrt(squared)
        distance = squared * inverse
        gain = count_buf[span, :] * inverse
        for f in range(freqs):
            sine, cosine = sincos_turns(distance * turns[f])
            cosine, sine = cosine * gain, sine * gain
            green_cos[f, span, :] = cosine
            green_sin[f, span, :] = sine
            real, imag = block[:, f : f + 1], block[:, freqs + f : freqs + f + 1]
            part_real = cosine * real - sine * imag
            part_imag = cosine * imag + sine * real
            eta_acc[f] += jnp.sum(part_real.reshape(STEP // 8, 8, points), axis=0)
            eta_acc[freqs + f] += jnp.sum(part_imag.reshape(STEP // 8, 8, points), axis=0)

    def field_block(r, carry):
        open_pack(src_pack, src_buf)(r, carry)
        for step in range(0, own, STEP):
            field_step(r * own + step)
        return carry

    def field_from(k, carry):
        panel_copy(k).wait_recv()
        return field_block(row_mate(k), carry)

    field_block(row, 0)
    lax.fori_loop(1, rows, field_from, 0)
    eta_buf[col] = jnp.sum(eta_acc[...], axis=1)
    eta_copies = [
        push(1, eta_buf.at[col], eta_buf.at[col], col_peer(k), col_sems, k)
        for k in range(1, cols)
    ]

    for copy in side:
        copy.wait_recv()
    lax.fori_loop(0, cols, open_pack(tgt_pack, tgt_buf), 0)
    src_rows[...] = jnp.transpose(src_buf[...])
    place = [src_rows[pos_at + axis : pos_at + axis + 1, :] for axis in range(3)]

    def gaps(block):
        return [block[:, pos_at + axis : pos_at + axis + 1] - place[axis] for axis in range(3)]

    def lengths(offset):
        squared = offset[0] * offset[0] + offset[1] * offset[1] + offset[2] * offset[2] + SOFT
        inverse = lax.rsqrt(squared)
        return squared * inverse, inverse

    def derivative(f, distance, inverse):
        inverse_cube = inverse * inverse * inverse
        phase = distance * waves[f]
        sine, cosine = sincos_turns(distance * turns[f])
        return -(cosine + phase * sine) * inverse_cube, (phase * cosine - sine) * inverse_cube

    if keep:

        def deriv_step(step, carry):
            span = pl.ds(pl.multiple_of(step * STEP, STEP), STEP)
            distance, inverse = lengths(gaps(tgt_buf[span, :]))
            for f in range(freqs):
                real, imag = derivative(f, distance, inverse)
                deriv_re[f, span, :] = real
                deriv_im[f, span, :] = imag
            return carry

        lax.fori_loop(0, targets // STEP // 2, deriv_step, 0)

    for copy in eta_copies:
        copy.wait_recv()
    eta = eta_buf[0]
    for k in range(1, cols):
        eta = eta + eta_buf[k]
    resid = eta - targ_ref[...]
    resid_buf[...] = resid
    misfit = jnp.sum(jnp.sum(resid * resid, axis=0, keepdims=True), axis=1, keepdims=True)
    lane = lax.broadcasted_iota(jnp.int32, (STEP, LANES), 1)

    def source_sums(start):
        span = pl.ds(pl.multiple_of(start, STEP), STEP)
        total = jnp.zeros((STEP, LANES), jnp.float32)
        for f in range(freqs):
            cosine, sine = green_cos[f, span, :], green_sin[f, span, :]
            real = resid_buf[f : f + 1, :]
            imag = resid_buf[freqs + f : freqs + f + 1, :]
            sum_real = jnp.sum(cosine * real + sine * imag, axis=1, keepdims=True)
            sum_imag = jnp.sum(cosine * imag - sine * real, axis=1, keepdims=True)
            total = jnp.where(lane == f, sum_real, total)
            total = jnp.where(lane == freqs + f, sum_imag, total)
        return total

    def source_block(r):
        sums = [source_sums(r * own + step) for step in range(0, own, STEP)]
        return pack(jnp.concatenate(sums, axis=0))

    misfit_rows = jnp.broadcast_to(misfit, (part, LANES))

    def source_copy(k):
        there = slot(row_mate(jnp.int32(k)), 2 * part, 2 * part)
        return describe(
            1, send_source.at[there], recv_source.at[src_mine], row_peer(k), row_sems, k
        )

    def source_step(step, carry):
        k = rows - step
        r = row_mate(k)
        send_source[slot(r, 2 * part, 2 * part), :] = jnp.concatenate(
            [source_block(r), misfit_rows], axis=0
        )
        source_copy(k).start()
        return carry

    lax.fori_loop(1, rows, source_step, 0)
    recv_source[src_mine, :] = jnp.concatenate([source_block(row), misfit_rows], axis=0)
    if keep:

        def turn_step(step, carry):
            span = pl.ds(pl.multiple_of(step * STEP, STEP), STEP)
            block = tgt_buf[span, :]
            for f in range(freqs):
                g = freqs + f
                real, imag = deriv_re[f, span, :], deriv_im[f, span, :]
                t_real, t_imag = block[:, f : f + 1], block[:, g : g + 1]
                s_real, s_imag = src_rows[f : f + 1, :], src_rows[g : g + 1, :]
                turned_re[f, span, :] = t_real * real - t_imag * imag
                turned_im[f, span, :] = t_real * imag + t_imag * real
                deriv_re[f, span, :] = s_real * real - s_imag * imag
                deriv_im[f, span, :] = s_real * imag + s_imag * real
            return carry

        lax.fori_loop(targets // STEP // 2, targets // STEP, deriv_step, 0)
        lax.fori_loop(0, targets // STEP, turn_step, 0)
    base = row * targets
    vertex = lax.broadcasted_iota(jnp.int32, (targets, targets), 0) + base
    share = jnp.zeros((targets, targets), jnp.float32)
    for corner in range(4):
        share = share + jnp.where(conn_ref[corner : corner + 1, :] == vertex, 0.25, 0.0)
    for k in range(1, rows):
        source_copy(k).wait_recv()
    both = recv_source[0 : 2 * part, :]
    for r in range(1, rows):
        both = both + recv_source[r * 2 * part : (r + 1) * 2 * part, :]
    objective = both[part : part + 1, 0:1] / (freqs * points * rows) + 1e-06
    obj_out[...] = objective
    source = unpack(both[0:part, :] / objective, 0)
    low = wide < freqs
    inv_own = pltpu.roll(mine, LANES - inv_at, 1)
    inv_turn = jnp.where(low, -pltpu.roll(inv_own, LANES - freqs, 1), pltpu.roll(inv_own, freqs, 1))
    real = jnp.where(low, source, pltpu.roll(source, freqs, 1))
    imag = jnp.where(low, pltpu.roll(source, LANES - freqs, 1), source)
    mu = jnp.where(wide < 2 * freqs, real * inv_own + imag * inv_turn, 0.0)
    packed = pack(mu)
    mu_row, mu_col = slot(row, part, part), slot(col, part, part)
    mu_src_pack[mu_row, :] = packed
    mu_tgt_pack[mu_col, :] = packed
    mu_copies = [
        push(2, mu_src_pack.at[mu_row], mu_src_pack.at[mu_row], row_peer(k), row_sems, k)
        for k in range(rows - 1, 0, -1)
    ] + [
        push(2, mu_tgt_pack.at[mu_col], mu_tgt_pack.at[mu_col], col_peer(k), col_sems, k)
        for k in range(1, cols)
    ]
    square_buf[0:own, :] = mu
    adj_out[...] = jnp.transpose(square_buf[...])[0 : 2 * freqs, 0:own]
    for copy in mu_copies:
        copy.wait_recv()

    def open_mu(packs, opened):
        def open_step(block, carry):
            opened[slot(block, own, own), :] = unpack(packs[slot(block, part, part), :], 0)
            return carry

        return open_step

    lax.fori_loop(0, rows, open_mu(mu_src_pack, mu_src), 0)
    lax.fori_loop(0, cols, open_mu(mu_tgt_pack, mu_tgt), 0)
    mu_rows[...] = jnp.transpose(mu_src[...])
    scale = 1.0 / math.sqrt(sources * cols * freqs)
    lane = lax.broadcasted_iota(jnp.int32, (STEP, LANES), 1)

    def sens_step(step, carry):
        span = pl.ds(pl.multiple_of(step * STEP, STEP), STEP)
        block, tmu = tgt_buf[span, :], mu_tgt[span, :]
        offset = gaps(block)
        distance, inverse = lengths(offset)
        weight = jnp.zeros((STEP, sources), jnp.float32)
        for f in range(freqs):
            g = freqs + f
            tm_real, tm_imag = tmu[:, f : f + 1], tmu[:, g : g + 1]
            sm_real, sm_imag = mu_rows[f : f + 1, :], mu_rows[g : g + 1, :]
            if keep:
                weight = weight + (tm_real * deriv_re[f, span, :] - tm_imag * deriv_im[f, span, :])
                weight = weight + (sm_real * turned_re[f, span, :] - sm_imag * turned_im[f, span, :])
                continue
            der_real, der_imag = derivative(f, distance, inverse)
            t_real, t_imag = block[:, f : f + 1], block[:, g : g + 1]
            s_real, s_imag = src_rows[f : f + 1, :], src_rows[g : g + 1, :]
            prod_real = tm_real * s_real - tm_imag * s_imag + sm_real * t_real - sm_imag * t_imag
            prod_imag = tm_real * s_imag + tm_imag * s_real + sm_real * t_imag + sm_imag * t_real
            weight = weight + (prod_real * der_real - prod_imag * der_imag)
        total = jnp.zeros((STEP, LANES), jnp.float32)
        for axis in range(3):
            part = jnp.sum(weight * offset[axis], axis=1, keepdims=True)
            total = jnp.where(lane == axis, part * scale, total)
        sens_buf[span, :] = total
        return carry

    lax.fori_loop(0, targets // STEP, sens_step, 0)
    vert_send[...] = jnp.dot(
        share,
        sens_buf[...],
        preferred_element_type=jnp.float32,
        precision=lax.Precision.HIGHEST,
    )
    vert_copies = []
    for k in range(1, cols):
        there = pl.ds(pl.multiple_of(lax.rem(col + k, cols) * own, own), own)
        vert_copies.append(
            push(3, vert_send.at[there], vert_recv.at[own_tgt], col_peer(k), col_sems, k)
        )
    vert_recv[own_tgt, :] = vert_send[own_tgt, :]
    for copy in vert_copies:
        copy.wait_recv()
    total = vert_recv[0:own, :]
    for k in range(1, cols):
        total = total + vert_recv[k * own : (k + 1) * own, :]
    square_buf[0:own, :] = total
    vert_out[...] = jnp.transpose(square_buf[...])[0:3, 0:own]
    for copy in side + eta_copies + mu_copies + vert_copies:
        copy.wait_send()
    for k in range(1, rows):
        panel_copy(k).wait_send()
        source_copy(k).wait_send()


def on_device(centroids, strengths, self_inv, wavenumbers, field_pos, targets, lists, connect):
    own = centroids.shape[1]
    rows, cols = lax.axis_size("row"), lax.axis_size("col")
    freqs = wavenumbers.shape[0]
    points, listed = lists.shape
    pack_rows = 2 * own * 2 * freqs // LANES
    sources, block = rows * own, cols * own
    keep = freqs * block * sources * 8 <= 16 * 2**20
    kept = (freqs, block, sources) if keep else (1, 8, LANES)
    f32 = jnp.float32
    vmem = pl.BlockSpec(memory_space=pltpu.VMEM)
    hbm = pl.BlockSpec(memory_space=pltpu.HBM)
    smem = pl.BlockSpec(memory_space=pltpu.SMEM)
    adjoint, vertex, objective = pl.pallas_call(
        functools.partial(kernel, (rows, cols, own, freqs, points, listed, keep)),
        out_shape=(
            jax.ShapeDtypeStruct((2 * freqs, own), f32),
            jax.ShapeDtypeStruct((3, own), f32),
            jax.ShapeDtypeStruct((1, 1), f32),
        ),
        in_specs=[hbm, hbm, hbm, smem, hbm, hbm, hbm, hbm],
        out_specs=(vmem, vmem, vmem),
        scratch_shapes=[
            pltpu.VMEM((LANES, LANES), f32),
            pltpu.VMEM((rows * pack_rows, LANES), f32),
            pltpu.VMEM((cols * pack_rows, LANES), f32),
            pltpu.VMEM((sources, LANES), f32),
            pltpu.VMEM((block, LANES), f32),
            pltpu.VMEM((LANES, sources), f32),
            pltpu.VMEM((listed, points), f32),
            pltpu.VMEM((sources, points), f32),
            pltpu.VMEM((freqs, sources, points), f32),
            pltpu.VMEM((freqs, sources, points), f32),
            pltpu.VMEM((2 * freqs, 8, points), f32),
            pltpu.VMEM((cols, 2 * freqs, points), f32),
            pltpu.VMEM((2 * freqs, points), f32),
            pltpu.VMEM((rows * pack_rows, LANES), f32),
            pltpu.VMEM((rows * pack_rows, LANES), f32),
            pltpu.VMEM((rows * pack_rows // 2, LANES), f32),
            pltpu.VMEM((cols * pack_rows // 2, LANES), f32),
            pltpu.VMEM((sources, LANES), f32),
            pltpu.VMEM((block, LANES), f32),
            pltpu.VMEM((LANES, sources), f32),
            pltpu.VMEM(kept, f32),
            pltpu.VMEM(kept, f32),
            pltpu.VMEM(kept, f32),
            pltpu.VMEM(kept, f32),
            pltpu.VMEM((block, LANES), f32),
            pltpu.VMEM((block, LANES), f32),
            pltpu.VMEM((block, LANES), f32),
            pltpu.SemaphoreType.DMA((3, rows)),
            pltpu.SemaphoreType.DMA((3, rows)),
            pltpu.SemaphoreType.DMA((4, cols)),
            pltpu.SemaphoreType.DMA((4, cols)),
            pltpu.VMEM(centroids.shape, f32),
            pltpu.VMEM(strengths.shape, f32),
            pltpu.VMEM(self_inv.shape, f32),
            pltpu.VMEM(field_pos.shape, f32),
            pltpu.VMEM(targets.shape, f32),
            pltpu.VMEM((listed, points), jnp.int32),
            pltpu.VMEM(connect.shape, jnp.int32),
            pltpu.SemaphoreType.DMA((7,)),
        ],
        compiler_params=pltpu.CompilerParams(
            collective_id=0, has_side_effects=True, vmem_limit_bytes=60 * 2**20
        ),
    )(centroids, strengths, self_inv, wavenumbers, field_pos, targets, lists.T, connect)
    return adjoint, vertex, objective.reshape(())


def solution(mesh):
    return jax.shard_map(
        on_device,
        mesh=mesh,
        in_specs=(
            P(None, ("row", "col")),
            P(None, ("row", "col")),
            P(None, ("row", "col")),
            P(),
            P(None, "row"),
            P(None, "row"),
            P("row", None),
            P(None, "row"),
        ),
        out_specs=(P(None, ("row", "col")), P(None, ("row", "col")), P()),
        check_vma=False,
    )
```

```python
import functools
import math

import jax
import jax.numpy as jnp
from jax import lax
from jax.experimental import pallas as pl
from jax.experimental.pallas import tpu as pltpu
from jax.sharding import PartitionSpec as P

SOFT = 1.0
LANES = 128
STEP = 16
MESH = pl.DeviceIdType.MESH
SIN_COEF = (6.283182818550509, -41.34142139863338, 81.59618387150631, -76.58010050947591, 41.205394790207706, -12.27126223106381)
COS_COEF = (0.999999221570582, -19.73898251610168, 64.92872660897218, -85.2723968955171, 58.7940381912709, -21.076781284621926)
MAGIC = 12582912.0


def horner(coefs, x):
    total = jnp.full_like(x, coefs[-1])
    for coef in coefs[-2::-1]:
        total = total * x + coef
    return total


def sincos_turns(turns):
    part = turns - ((turns + MAGIC) - MAGIC)
    square = part * part
    return part * horner(SIN_COEF, square), horner(COS_COEF, square)


def kernel(
    dims,
    cen_hbm,
    str_hbm,
    inv_hbm,
    wave_ref,
    field_hbm,
    targ_hbm,
    lists_hbm,
    conn_hbm,
    adj_out,
    vert_out,
    obj_out,
    square_buf,
    src_pack,
    tgt_pack,
    src_buf,
    tgt_buf,
    src_rows,
    list_rows,
    count_buf,
    green_cos,
    green_sin,
    eta_acc,
    eta_buf,
    resid_buf,
    send_source,
    recv_source,
    mu_src_pack,
    mu_tgt_pack,
    mu_src,
    mu_tgt,
    mu_rows,
    deriv_re,
    deriv_im,
    turned_re,
    turned_im,
    weight_buf,
    sens_buf,
    vert_send,
    vert_recv,
    send_row,
    recv_row,
    send_col,
    recv_col,
    cen_ref,
    str_ref,
    inv_ref,
    field_ref,
    targ_ref,
    lists_ref,
    conn_ref,
    load_sem,
):
    rows, cols, own, freqs, points, listed, keep = dims
    sources, targets = rows * own, cols * own
    pos_at, inv_at = 2 * freqs, 2 * freqs + 8
    row, col = lax.axis_index("row"), lax.axis_index("col")

    loads = [
        pltpu.make_async_copy(there, here, load_sem.at[index])
        for index, (there, here) in enumerate(
            [
                (cen_hbm, cen_ref),
                (str_hbm, str_ref),
                (inv_hbm, inv_ref),
                (lists_hbm, lists_ref),
                (field_hbm, field_ref),
                (targ_hbm, targ_ref),
                (conn_hbm, conn_ref),
            ]
        )
    ]
    for load in loads:
        load.start()

    if rows & (rows - 1):
        raise ValueError("rows")

    def row_mate(k):
        mate, bit = 0, 1
        while bit < rows:
            mate = mate + bit * lax.rem(lax.div(row, bit) + lax.div(k, bit), 2)
            bit *= 2
        return mate

    def row_peer(k):
        return (row_mate(jnp.int32(k)), col)

    def col_peer(k):
        return (row, lax.rem(col + k, cols))

    barrier = pltpu.get_barrier_semaphore()
    for k in range(1, rows):
        pl.semaphore_signal(barrier, inc=1, device_id=row_peer(k), device_id_type=MESH)
    for k in range(1, cols):
        pl.semaphore_signal(barrier, inc=1, device_id=col_peer(k), device_id_type=MESH)

    own_tgt = pl.ds(pl.multiple_of(col * own, own), own)
    groups = LANES // (2 * freqs)
    part = own // groups

    def slot(index, size, depth):
        return pl.ds(pl.multiple_of(index * depth, depth), size)

    def pack(block):
        total = block[0:part, :]
        for g in range(1, groups):
            total = total + pltpu.roll(block[g * part : (g + 1) * part, :], g * 2 * freqs, 1)
        return total

    def unpack(block, shift):
        parts = []
        for g in range(groups):
            by = (shift - g * 2 * freqs) % LANES
            parts.append(pltpu.roll(block, by, 1) if by else block)
        return jnp.concatenate(parts, axis=0)

    wide = lax.broadcasted_iota(jnp.int32, (own, LANES), 1)

    square_buf[...] = jnp.zeros_like(square_buf)
    for load in loads[:3]:
        load.wait()
    square_buf[0 : 2 * freqs, 0:own] = str_ref[...]
    square_buf[pos_at : pos_at + 3, 0:own] = cen_ref[...]
    square_buf[inv_at : inv_at + 2 * freqs, 0:own] = inv_ref[...]
    mine = jnp.transpose(square_buf[...])[0:own, :]
    packed = jnp.concatenate(
        [
            pack(jnp.where(wide < pos_at, mine, 0.0)),
            pack(jnp.where(wide < 8, pltpu.roll(mine, LANES - pos_at, 1), 0.0)),
        ],
        axis=0,
    )
    src_mine, tgt_mine = slot(row, 2 * part, 2 * part), slot(col, 2 * part, 2 * part)
    src_pack[src_mine, :] = packed
    tgt_pack[tgt_mine, :] = packed

    def describe(stage, source, target, peer, sems, k):
        return pltpu.make_async_remote_copy(
            src_ref=source,
            dst_ref=target,
            send_sem=sems[0].at[stage, k],
            recv_sem=sems[1].at[stage, k],
            device_id=peer,
            device_id_type=MESH,
        )

    def push(*what):
        copy = describe(*what)
        copy.start()
        return copy

    row_sems, col_sems = (send_row, recv_row), (send_col, recv_col)
    pl.semaphore_wait(barrier, rows + cols - 2)

    def panel_copy(k):
        return describe(
            0, src_pack.at[src_mine], src_pack.at[src_mine], row_peer(k), row_sems, k
        )

    for k in range(rows - 1, 0, -1):
        panel_copy(k).start()
    side = [
        push(0, tgt_pack.at[tgt_mine], tgt_pack.at[tgt_mine], col_peer(k), col_sems, k)
        for k in range(1, cols)
    ]

    for load in loads[3:]:
        load.wait()
    list_rows[...] = lists_ref[...].astype(jnp.float32)

    def count_step(block, carry):
        start = pl.multiple_of(block * own, own)
        ids = lax.broadcasted_iota(jnp.int32, (own, points), 0) + (block * cols + col) * own
        ids = ids.astype(jnp.float32)
        total = jnp.zeros((own, points), jnp.float32)
        for entry in range(listed):
            total = total + jnp.where(list_rows[entry : entry + 1, :] == ids, 1.0, 0.0)
        count_buf[pl.ds(start, own), :] = total
        return carry

    lax.fori_loop(0, rows, count_step, 0)
    eta_acc[...] = jnp.zeros_like(eta_acc)
    field = [field_ref[axis : axis + 1, :] for axis in range(3)]
    waves = [wave_ref[f] for f in range(freqs)]
    turns = [wave * (0.5 / math.pi) for wave in waves]

    def open_pack(packs, opened):
        def open_step(block, carry):
            both = packs[slot(block, 2 * part, 2 * part), :]
            strength, place = unpack(both[0:part, :], 0), unpack(both[part:, :], pos_at)
            opened[slot(block, own, own), :] = jnp.where(wide < pos_at, strength, place)
            return carry

        return open_step


    def field_step(start):
        span = pl.ds(pl.multiple_of(start, STEP), STEP)
        block = src_buf[span, :]
        squared = SOFT
        for axis in range(3):
            gap = field[axis] - block[:, pos_at + axis : pos_at + axis + 1]
            squared = gap * gap + squared
        inverse = lax.rsqrt(squared)
        distance = squared * inverse
        gain = count_buf[span, :] * inverse
        for f in range(freqs):
            sine, cosine = sincos_turns(distance * turns[f])
            cosine, sine = cosine * gain, sine * gain
            green_cos[f, span, :] = cosine
            green_sin[f, span, :] = sine
            real, imag = block[:, f : f + 1], block[:, freqs + f : freqs + f + 1]
            part_real = cosine * real - sine * imag
            part_imag = cosine * imag + sine * real
            eta_acc[f] += jnp.sum(part_real.reshape(STEP // 8, 8, points), axis=0)
            eta_acc[freqs + f] += jnp.sum(part_imag.reshape(STEP // 8, 8, points), axis=0)

    def field_block(r, carry):
        open_pack(src_pack, src_buf)(r, carry)
        for step in range(0, own, STEP):
            field_step(r * own + step)
        return carry

    def field_from(k, carry):
        panel_copy(k).wait_recv()
        return field_block(row_mate(k), carry)

    field_block(row, 0)
    lax.fori_loop(1, rows, field_from, 0)
    eta_buf[col] = jnp.sum(eta_acc[...], axis=1)
    eta_copies = [
        push(1, eta_buf.at[col], eta_buf.at[col], col_peer(k), col_sems, k)
        for k in range(1, cols)
    ]

    for copy in side:
        copy.wait_recv()
    lax.fori_loop(0, cols, open_pack(tgt_pack, tgt_buf), 0)
    src_rows[...] = jnp.transpose(src_buf[...])
    place = [src_rows[pos_at + axis : pos_at + axis + 1, :] for axis in range(3)]

    def gaps(block):
        return [block[:, pos_at + axis : pos_at + axis + 1] - place[axis] for axis in range(3)]

    def lengths(offset):
        squared = offset[0] * offset[0] + offset[1] * offset[1] + offset[2] * offset[2] + SOFT
        inverse = lax.rsqrt(squared)
        return squared * inverse, inverse

    def derivative(f, distance, inverse):
        inverse_cube = inverse * inverse * inverse
        phase = distance * waves[f]
        sine, cosine = sincos_turns(distance * turns[f])
        return -(cosine + phase * sine) * inverse_cube, (phase * cosine - sine) * inverse_cube

    if keep:

        def deriv_step(step, carry):
            span = pl.ds(pl.multiple_of(step * STEP, STEP), STEP)
            distance, inverse = lengths(gaps(tgt_buf[span, :]))
            for f in range(freqs):
                real, imag = derivative(f, distance, inverse)
                deriv_re[f, span, :] = real
                deriv_im[f, span, :] = imag
            return carry

        lax.fori_loop(0, targets // STEP // 2, deriv_step, 0)

    for copy in eta_copies:
        copy.wait_recv()
    eta = eta_buf[0]
    for k in range(1, cols):
        eta = eta + eta_buf[k]
    resid = eta - targ_ref[...]
    resid_buf[...] = resid
    misfit = jnp.sum(jnp.sum(resid * resid, axis=0, keepdims=True), axis=1, keepdims=True)
    lane = lax.broadcasted_iota(jnp.int32, (STEP, LANES), 1)

    def source_sums(start):
        span = pl.ds(pl.multiple_of(start, STEP), STEP)
        total = jnp.zeros((STEP, LANES), jnp.float32)
        for f in range(freqs):
            cosine, sine = green_cos[f, span, :], green_sin[f, span, :]
            real = resid_buf[f : f + 1, :]
            imag = resid_buf[freqs + f : freqs + f + 1, :]
            sum_real = jnp.sum(cosine * real + sine * imag, axis=1, keepdims=True)
            sum_imag = jnp.sum(cosine * imag - sine * real, axis=1, keepdims=True)
            total = jnp.where(lane == f, sum_real, total)
            total = jnp.where(lane == freqs + f, sum_imag, total)
        return total

    def source_block(r):
        sums = [source_sums(r * own + step) for step in range(0, own, STEP)]
        return pack(jnp.concatenate(sums, axis=0))

    misfit_rows = jnp.broadcast_to(misfit, (part, LANES))

    def source_copy(k):
        there = slot(row_mate(jnp.int32(k)), 2 * part, 2 * part)
        return describe(
            1, send_source.at[there], recv_source.at[src_mine], row_peer(k), row_sems, k
        )

    def source_step(step, carry):
        k = rows - step
        r = row_mate(k)
        send_source[slot(r, 2 * part, 2 * part), :] = jnp.concatenate(
            [source_block(r), misfit_rows], axis=0
        )
        source_copy(k).start()
        return carry

    lax.fori_loop(1, rows, source_step, 0)
    recv_source[src_mine, :] = jnp.concatenate([source_block(row), misfit_rows], axis=0)
    if keep:

        def turn_step(step, carry):
            span = pl.ds(pl.multiple_of(step * STEP, STEP), STEP)
            block = tgt_buf[span, :]
            for f in range(freqs):
                g = freqs + f
                real, imag = deriv_re[f, span, :], deriv_im[f, span, :]
                t_real, t_imag = block[:, f : f + 1], block[:, g : g + 1]
                s_real, s_imag = src_rows[f : f + 1, :], src_rows[g : g + 1, :]
                turned_re[f, span, :] = t_real * real - t_imag * imag
                turned_im[f, span, :] = t_real * imag + t_imag * real
                deriv_re[f, span, :] = s_real * real - s_imag * imag
                deriv_im[f, span, :] = s_real * imag + s_imag * real
            return carry

        lax.fori_loop(targets // STEP // 2, targets // STEP, deriv_step, 0)
        lax.fori_loop(0, targets // STEP, turn_step, 0)
    base = row * targets
    vertex = lax.broadcasted_iota(jnp.int32, (targets, targets), 0) + base
    share = jnp.zeros((targets, targets), jnp.float32)
    for corner in range(4):
        share = share + jnp.where(conn_ref[corner : corner + 1, :] == vertex, 0.25, 0.0)
    for k in range(1, rows):
        source_copy(k).wait_recv()
    both = recv_source[0 : 2 * part, :]
    for r in range(1, rows):
        both = both + recv_source[r * 2 * part : (r + 1) * 2 * part, :]
    objective = both[part : part + 1, 0:1] / (freqs * points * rows) + 1e-06
    obj_out[...] = objective
    source = unpack(both[0:part, :] / objective, 0)
    low = wide < freqs
    inv_own = pltpu.roll(mine, LANES - inv_at, 1)
    inv_turn = jnp.where(low, -pltpu.roll(inv_own, LANES - freqs, 1), pltpu.roll(inv_own, freqs, 1))
    real = jnp.where(low, source, pltpu.roll(source, freqs, 1))
    imag = jnp.where(low, pltpu.roll(source, LANES - freqs, 1), source)
    mu = jnp.where(wide < 2 * freqs, real * inv_own + imag * inv_turn, 0.0)
    packed = pack(mu)
    mu_row, mu_col = slot(row, part, part), slot(col, part, part)
    mu_src_pack[mu_row, :] = packed
    mu_tgt_pack[mu_col, :] = packed
    mu_copies = [
        push(2, mu_src_pack.at[mu_row], mu_src_pack.at[mu_row], row_peer(k), row_sems, k)
        for k in range(rows - 1, 0, -1)
    ] + [
        push(2, mu_tgt_pack.at[mu_col], mu_tgt_pack.at[mu_col], col_peer(k), col_sems, k)
        for k in range(1, cols)
    ]
    square_buf[0:own, :] = mu
    adj_out[...] = jnp.transpose(square_buf[...])[0 : 2 * freqs, 0:own]
    def open_mu(packs, opened):
        def open_step(block, carry):
            opened[slot(block, own, own), :] = unpack(packs[slot(block, part, part), :], 0)
            return carry

        return open_step

    for copy in mu_copies[rows - 1 :]:
        copy.wait_recv()
    lax.fori_loop(0, cols, open_mu(mu_tgt_pack, mu_tgt), 0)
    if keep:

        def first_step(step, carry):
            span = pl.ds(pl.multiple_of(step * STEP, STEP), STEP)
            tmu = mu_tgt[span, :]
            weight = jnp.zeros((STEP, sources), jnp.float32)
            for f in range(freqs):
                g = freqs + f
                tm_real, tm_imag = tmu[:, f : f + 1], tmu[:, g : g + 1]
                weight = weight + (tm_real * deriv_re[f, span, :] - tm_imag * deriv_im[f, span, :])
            weight_buf[span, :] = weight
            return carry

        lax.fori_loop(0, targets // STEP, first_step, 0)
    for copy in mu_copies[: rows - 1]:
        copy.wait_recv()
    lax.fori_loop(0, rows, open_mu(mu_src_pack, mu_src), 0)
    mu_rows[...] = jnp.transpose(mu_src[...])
    scale = 1.0 / math.sqrt(sources * cols * freqs)
    lane = lax.broadcasted_iota(jnp.int32, (STEP, LANES), 1)

    def sens_step(step, carry):
        span = pl.ds(pl.multiple_of(step * STEP, STEP), STEP)
        block, tmu = tgt_buf[span, :], mu_tgt[span, :]
        offset = gaps(block)
        distance, inverse = lengths(offset)
        weight = weight_buf[span, :] if keep else jnp.zeros((STEP, sources), jnp.float32)
        for f in range(freqs):
            g = freqs + f
            sm_real, sm_imag = mu_rows[f : f + 1, :], mu_rows[g : g + 1, :]
            if keep:
                weight = weight + (sm_real * turned_re[f, span, :] - sm_imag * turned_im[f, span, :])
                continue
            der_real, der_imag = derivative(f, distance, inverse)
            tm_real, tm_imag = tmu[:, f : f + 1], tmu[:, g : g + 1]
            t_real, t_imag = block[:, f : f + 1], block[:, g : g + 1]
            s_real, s_imag = src_rows[f : f + 1, :], src_rows[g : g + 1, :]
            prod_real = tm_real * s_real - tm_imag * s_imag + sm_real * t_real - sm_imag * t_imag
            prod_imag = tm_real * s_imag + tm_imag * s_real + sm_real * t_imag + sm_imag * t_real
            weight = weight + (prod_real * der_real - prod_imag * der_imag)
        total = jnp.zeros((STEP, LANES), jnp.float32)
        for axis in range(3):
            part = jnp.sum(weight * offset[axis], axis=1, keepdims=True)
            total = jnp.where(lane == axis, part * scale, total)
        sens_buf[span, :] = total
        return carry

    lax.fori_loop(0, targets // STEP, sens_step, 0)
    vert_send[...] = lax.dot_general(
        jnp.transpose(sens_buf[...])[0:8, :],
        share,
        (((1,), (1,)), ((), ())),
        preferred_element_type=jnp.float32,
        precision=lax.Precision.HIGHEST,
    )
    per_group = LANES // own

    def vert_group(c):
        start = lax.div(c, per_group) * LANES
        return vert_send.at[:, pl.ds(pl.multiple_of(start, LANES), LANES)]

    vert_mine = slot(col, 8, 8)
    vert_copies = [
        push(
            3, vert_group(lax.rem(col + k, cols)), vert_recv.at[vert_mine], col_peer(k), col_sems, k
        )
        for k in range(1, cols)
    ]
    vert_recv[vert_mine, :] = vert_group(col)[...]
    for copy in vert_copies:
        copy.wait_recv()
    total = vert_recv[0:8, :]
    for k in range(1, cols):
        total = total + vert_recv[k * 8 : (k + 1) * 8, :]
    place_in = lax.rem(col, per_group)
    vertex_own = total
    for spot in range(1, per_group):
        vertex_own = jnp.where(place_in == spot, pltpu.roll(total, LANES - spot * own, 1), vertex_own)
    vert_out[...] = vertex_own[0:3, 0:own]
    for copy in side + eta_copies + mu_copies + vert_copies:
        copy.wait_send()
    for k in range(1, rows):
        panel_copy(k).wait_send()
        source_copy(k).wait_send()


def on_device(centroids, strengths, self_inv, wavenumbers, field_pos, targets, lists, connect):
    own = centroids.shape[1]
    rows, cols = lax.axis_size("row"), lax.axis_size("col")
    freqs = wavenumbers.shape[0]
    points, listed = lists.shape
    pack_rows = 2 * own * 2 * freqs // LANES
    sources, block = rows * own, cols * own
    keep = freqs * block * sources * 8 <= 16 * 2**20
    kept = (freqs, block, sources) if keep else (1, 8, LANES)
    f32 = jnp.float32
    vmem = pl.BlockSpec(memory_space=pltpu.VMEM)
    hbm = pl.BlockSpec(memory_space=pltpu.HBM)
    smem = pl.BlockSpec(memory_space=pltpu.SMEM)
    adjoint, vertex, objective = pl.pallas_call(
        functools.partial(kernel, (rows, cols, own, freqs, points, listed, keep)),
        out_shape=(
            jax.ShapeDtypeStruct((2 * freqs, own), f32),
            jax.ShapeDtypeStruct((3, own), f32),
            jax.ShapeDtypeStruct((1, 1), f32),
        ),
        in_specs=[hbm, hbm, hbm, smem, hbm, hbm, hbm, hbm],
        out_specs=(vmem, vmem, vmem),
        scratch_shapes=[
            pltpu.VMEM((LANES, LANES), f32),
            pltpu.VMEM((rows * pack_rows, LANES), f32),
            pltpu.VMEM((cols * pack_rows, LANES), f32),
            pltpu.VMEM((sources, LANES), f32),
            pltpu.VMEM((block, LANES), f32),
            pltpu.VMEM((LANES, sources), f32),
            pltpu.VMEM((listed, points), f32),
            pltpu.VMEM((sources, points), f32),
            pltpu.VMEM((freqs, sources, points), f32),
            pltpu.VMEM((freqs, sources, points), f32),
            pltpu.VMEM((2 * freqs, 8, points), f32),
            pltpu.VMEM((cols, 2 * freqs, points), f32),
            pltpu.VMEM((2 * freqs, points), f32),
            pltpu.VMEM((rows * pack_rows, LANES), f32),
            pltpu.VMEM((rows * pack_rows, LANES), f32),
            pltpu.VMEM((rows * pack_rows // 2, LANES), f32),
            pltpu.VMEM((cols * pack_rows // 2, LANES), f32),
            pltpu.VMEM((sources, LANES), f32),
            pltpu.VMEM((block, LANES), f32),
            pltpu.VMEM((LANES, sources), f32),
            pltpu.VMEM(kept, f32),
            pltpu.VMEM(kept, f32),
            pltpu.VMEM(kept, f32),
            pltpu.VMEM(kept, f32),
            pltpu.VMEM(kept[1:], f32),
            pltpu.VMEM((block, LANES), f32),
            pltpu.VMEM((8, block), f32),
            pltpu.VMEM((cols * 8, LANES), f32),
            pltpu.SemaphoreType.DMA((3, rows)),
            pltpu.SemaphoreType.DMA((3, rows)),
            pltpu.SemaphoreType.DMA((4, cols)),
            pltpu.SemaphoreType.DMA((4, cols)),
            pltpu.VMEM(centroids.shape, f32),
            pltpu.VMEM(strengths.shape, f32),
            pltpu.VMEM(self_inv.shape, f32),
            pltpu.VMEM(field_pos.shape, f32),
            pltpu.VMEM(targets.shape, f32),
            pltpu.VMEM((listed, points), jnp.int32),
            pltpu.VMEM(connect.shape, jnp.int32),
            pltpu.SemaphoreType.DMA((7,)),
        ],
        compiler_params=pltpu.CompilerParams(
            collective_id=0, has_side_effects=True, vmem_limit_bytes=60 * 2**20
        ),
    )(centroids, strengths, self_inv, wavenumbers, field_pos, targets, lists.T, connect)
    return adjoint, vertex, objective.reshape(())


def solution(mesh):
    return jax.shard_map(
        on_device,
        mesh=mesh,
        in_specs=(
            P(None, ("row", "col")),
            P(None, ("row", "col")),
            P(None, ("row", "col")),
            P(),
            P(None, "row"),
            P(None, "row"),
            P("row", None),
            P(None, "row"),
        ),
        out_specs=(P(None, ("row", "col")), P(None, ("row", "col")), P()),
        check_vma=False,
    )
```

```python
import functools
import math

import jax
import jax.numpy as jnp
from jax import lax
from jax.experimental import pallas as pl
from jax.experimental.pallas import tpu as pltpu
from jax.sharding import PartitionSpec as P

SOFT = 1.0
LANES = 128
STEP = 16
MESH = pl.DeviceIdType.MESH
SIN_COEF = (6.283182818550509, -41.34142139863338, 81.59618387150631, -76.58010050947591, 41.205394790207706, -12.27126223106381)
COS_COEF = (0.999999221570582, -19.73898251610168, 64.92872660897218, -85.2723968955171, 58.7940381912709, -21.076781284621926)
MAGIC = 12582912.0


def horner(coefs, x):
    total = jnp.full_like(x, coefs[-1])
    for coef in coefs[-2::-1]:
        total = total * x + coef
    return total


def sincos_turns(turns):
    part = turns - ((turns + MAGIC) - MAGIC)
    square = part * part
    return part * horner(SIN_COEF, square), horner(COS_COEF, square)


def kernel(
    dims,
    cen_hbm,
    str_hbm,
    inv_hbm,
    wave_ref,
    field_hbm,
    targ_hbm,
    lists_hbm,
    conn_hbm,
    both_out,
    obj_out,
    square_buf,
    src_pack,
    tgt_pack,
    src_buf,
    tgt_buf,
    src_rows,
    list_rows,
    count_buf,
    green_cos,
    green_sin,
    eta_acc,
    eta_buf,
    resid_buf,
    send_source,
    recv_source,
    mu_src_pack,
    mu_tgt_pack,
    mu_src,
    mu_tgt,
    mu_rows,
    deriv_re,
    deriv_im,
    turned_re,
    turned_im,
    weight_buf,
    sens_buf,
    vert_send,
    vert_recv,
    send_row,
    recv_row,
    send_col,
    recv_col,
    cen_ref,
    str_ref,
    inv_ref,
    field_ref,
    targ_ref,
    lists_ref,
    conn_ref,
    load_sem,
):
    rows, cols, own, freqs, points, listed, keep = dims
    sources, targets = rows * own, cols * own
    pos_at, inv_at = 2 * freqs, 2 * freqs + 8
    row, col = lax.axis_index("row"), lax.axis_index("col")

    loads = [
        pltpu.make_async_copy(there, here, load_sem.at[index])
        for index, (there, here) in enumerate(
            [
                (cen_hbm, cen_ref),
                (str_hbm, str_ref),
                (inv_hbm, inv_ref),
                (lists_hbm, lists_ref),
                (field_hbm, field_ref),
                (targ_hbm, targ_ref),
                (conn_hbm, conn_ref),
            ]
        )
    ]
    for load in loads:
        load.start()

    if rows & (rows - 1):
        raise ValueError("rows")

    def row_mate(k):
        mate, bit = 0, 1
        while bit < rows:
            mate = mate + bit * lax.rem(lax.div(row, bit) + lax.div(k, bit), 2)
            bit *= 2
        return mate

    def row_peer(k):
        return (row_mate(jnp.int32(k)), col)

    def col_peer(k):
        return (row, lax.rem(col + k, cols))

    barrier = pltpu.get_barrier_semaphore()
    for k in range(1, rows):
        pl.semaphore_signal(barrier, inc=1, device_id=row_peer(k), device_id_type=MESH)
    for k in range(1, cols):
        pl.semaphore_signal(barrier, inc=1, device_id=col_peer(k), device_id_type=MESH)

    own_tgt = pl.ds(pl.multiple_of(col * own, own), own)
    groups = LANES // (2 * freqs)
    part = own // groups

    def slot(index, size, depth):
        return pl.ds(pl.multiple_of(index * depth, depth), size)

    def pack(block):
        total = block[0:part, :]
        for g in range(1, groups):
            total = total + pltpu.roll(block[g * part : (g + 1) * part, :], g * 2 * freqs, 1)
        return total

    def unpack(block, shift):
        parts = []
        for g in range(groups):
            by = (shift - g * 2 * freqs) % LANES
            parts.append(pltpu.roll(block, by, 1) if by else block)
        return jnp.concatenate(parts, axis=0)

    wide = lax.broadcasted_iota(jnp.int32, (own, LANES), 1)

    square_buf[...] = jnp.zeros_like(square_buf)
    for load in loads[:3]:
        load.wait()
    square_buf[0 : 2 * freqs, 0:own] = str_ref[...]
    square_buf[pos_at : pos_at + 3, 0:own] = cen_ref[...]
    square_buf[inv_at : inv_at + 2 * freqs, 0:own] = inv_ref[...]
    mine = jnp.transpose(square_buf[...])[0:own, :]
    packed = jnp.concatenate(
        [
            pack(jnp.where(wide < pos_at, mine, 0.0)),
            pack(jnp.where(wide < 8, pltpu.roll(mine, LANES - pos_at, 1), 0.0)),
        ],
        axis=0,
    )
    src_mine, tgt_mine = slot(row, 2 * part, 2 * part), slot(col, 2 * part, 2 * part)
    src_pack[src_mine, :] = packed
    tgt_pack[tgt_mine, :] = packed

    def describe(stage, source, target, peer, sems, k):
        return pltpu.make_async_remote_copy(
            src_ref=source,
            dst_ref=target,
            send_sem=sems[0].at[stage, k],
            recv_sem=sems[1].at[stage, k],
            device_id=peer,
            device_id_type=MESH,
        )

    def push(*what):
        copy = describe(*what)
        copy.start()
        return copy

    row_sems, col_sems = (send_row, recv_row), (send_col, recv_col)
    pl.semaphore_wait(barrier, rows + cols - 2)

    def panel_copy(k):
        return describe(
            0, src_pack.at[src_mine], src_pack.at[src_mine], row_peer(k), row_sems, k
        )

    for k in range(rows - 1, 0, -1):
        panel_copy(k).start()
    side = [
        push(0, tgt_pack.at[tgt_mine], tgt_pack.at[tgt_mine], col_peer(k), col_sems, k)
        for k in range(1, cols)
    ]

    for load in loads[3:]:
        load.wait()
    list_rows[...] = lists_ref[...].astype(jnp.float32)

    def count_step(block, carry):
        start = pl.multiple_of(block * own, own)
        ids = lax.broadcasted_iota(jnp.int32, (own, points), 0) + (block * cols + col) * own
        ids = ids.astype(jnp.float32)
        total = jnp.zeros((own, points), jnp.float32)
        for entry in range(listed):
            total = total + jnp.where(list_rows[entry : entry + 1, :] == ids, 1.0, 0.0)
        count_buf[pl.ds(start, own), :] = total
        return carry

    lax.fori_loop(0, rows, count_step, 0)
    eta_acc[...] = jnp.zeros_like(eta_acc)
    field = [field_ref[axis : axis + 1, :] for axis in range(3)]
    waves = [wave_ref[f] for f in range(freqs)]
    turns = [wave * (0.5 / math.pi) for wave in waves]

    def open_pack(packs, opened):
        def open_step(block, carry):
            both = packs[slot(block, 2 * part, 2 * part), :]
            strength, place = unpack(both[0:part, :], 0), unpack(both[part:, :], pos_at)
            opened[slot(block, own, own), :] = jnp.where(wide < pos_at, strength, place)
            return carry

        return open_step


    def field_step(start):
        span = pl.ds(pl.multiple_of(start, STEP), STEP)
        block = src_buf[span, :]
        squared = SOFT
        for axis in range(3):
            gap = field[axis] - block[:, pos_at + axis : pos_at + axis + 1]
            squared = gap * gap + squared
        inverse = lax.rsqrt(squared)
        distance = squared * inverse
        gain = count_buf[span, :] * inverse
        for f in range(freqs):
            sine, cosine = sincos_turns(distance * turns[f])
            cosine, sine = cosine * gain, sine * gain
            green_cos[f, span, :] = cosine
            green_sin[f, span, :] = sine
            real, imag = block[:, f : f + 1], block[:, freqs + f : freqs + f + 1]
            part_real = cosine * real - sine * imag
            part_imag = cosine * imag + sine * real
            eta_acc[f] += jnp.sum(part_real.reshape(STEP // 8, 8, points), axis=0)
            eta_acc[freqs + f] += jnp.sum(part_imag.reshape(STEP // 8, 8, points), axis=0)

    def field_block(r, carry):
        open_pack(src_pack, src_buf)(r, carry)
        for step in range(0, own, STEP):
            field_step(r * own + step)
        return carry

    def field_from(k, carry):
        panel_copy(k).wait_recv()
        return field_block(row_mate(k), carry)

    field_block(row, 0)
    lax.fori_loop(1, rows, field_from, 0)
    eta_buf[col] = jnp.sum(eta_acc[...], axis=1)
    eta_copies = [
        push(1, eta_buf.at[col], eta_buf.at[col], col_peer(k), col_sems, k)
        for k in range(1, cols)
    ]

    for copy in side:
        copy.wait_recv()
    lax.fori_loop(0, cols, open_pack(tgt_pack, tgt_buf), 0)
    src_rows[...] = jnp.transpose(src_buf[...])
    place = [src_rows[pos_at + axis : pos_at + axis + 1, :] for axis in range(3)]

    def gaps(block):
        return [block[:, pos_at + axis : pos_at + axis + 1] - place[axis] for axis in range(3)]

    def lengths(offset):
        squared = offset[0] * offset[0] + offset[1] * offset[1] + offset[2] * offset[2] + SOFT
        inverse = lax.rsqrt(squared)
        return squared * inverse, inverse

    def derivative(f, distance, inverse):
        inverse_cube = inverse * inverse * inverse
        phase = distance * waves[f]
        sine, cosine = sincos_turns(distance * turns[f])
        return -(cosine + phase * sine) * inverse_cube, (phase * cosine - sine) * inverse_cube

    if keep:

        def deriv_step(step, carry):
            span = pl.ds(pl.multiple_of(step * STEP, STEP), STEP)
            distance, inverse = lengths(gaps(tgt_buf[span, :]))
            for f in range(freqs):
                real, imag = derivative(f, distance, inverse)
                deriv_re[f, span, :] = real
                deriv_im[f, span, :] = imag
            return carry

        lax.fori_loop(0, targets // STEP // 2, deriv_step, 0)

    for copy in eta_copies:
        copy.wait_recv()
    eta = eta_buf[0]
    for k in range(1, cols):
        eta = eta + eta_buf[k]
    resid = eta - targ_ref[...]
    resid_buf[...] = resid
    misfit = jnp.sum(jnp.sum(resid * resid, axis=0, keepdims=True), axis=1, keepdims=True)
    lane = lax.broadcasted_iota(jnp.int32, (STEP, LANES), 1)

    def source_sums(start):
        span = pl.ds(pl.multiple_of(start, STEP), STEP)
        total = jnp.zeros((STEP, LANES), jnp.float32)
        for f in range(freqs):
            cosine, sine = green_cos[f, span, :], green_sin[f, span, :]
            real = resid_buf[f : f + 1, :]
            imag = resid_buf[freqs + f : freqs + f + 1, :]
            sum_real = jnp.sum(cosine * real + sine * imag, axis=1, keepdims=True)
            sum_imag = jnp.sum(cosine * imag - sine * real, axis=1, keepdims=True)
            total = jnp.where(lane == f, sum_real, total)
            total = jnp.where(lane == freqs + f, sum_imag, total)
        return total

    def source_block(r):
        sums = [source_sums(r * own + step) for step in range(0, own, STEP)]
        return pack(jnp.concatenate(sums, axis=0))

    misfit_rows = jnp.broadcast_to(misfit, (part, LANES))

    def source_copy(k):
        there = slot(row_mate(jnp.int32(k)), 2 * part, 2 * part)
        return describe(
            1, send_source.at[there], recv_source.at[src_mine], row_peer(k), row_sems, k
        )

    def source_step(step, carry):
        k = rows - step
        r = row_mate(k)
        send_source[slot(r, 2 * part, 2 * part), :] = jnp.concatenate(
            [source_block(r), misfit_rows], axis=0
        )
        source_copy(k).start()
        return carry

    lax.fori_loop(1, rows, source_step, 0)
    recv_source[src_mine, :] = jnp.concatenate([source_block(row), misfit_rows], axis=0)
    if keep:

        def turn_step(step, carry):
            span = pl.ds(pl.multiple_of(step * STEP, STEP), STEP)
            block = tgt_buf[span, :]
            for f in range(freqs):
                g = freqs + f
                real, imag = deriv_re[f, span, :], deriv_im[f, span, :]
                t_real, t_imag = block[:, f : f + 1], block[:, g : g + 1]
                s_real, s_imag = src_rows[f : f + 1, :], src_rows[g : g + 1, :]
                turned_re[f, span, :] = t_real * real - t_imag * imag
                turned_im[f, span, :] = t_real * imag + t_imag * real
                deriv_re[f, span, :] = s_real * real - s_imag * imag
                deriv_im[f, span, :] = s_real * imag + s_imag * real
            return carry

        lax.fori_loop(targets // STEP // 2, targets // STEP, deriv_step, 0)
        lax.fori_loop(0, targets // STEP, turn_step, 0)
    base = row * targets
    vertex = lax.broadcasted_iota(jnp.int32, (targets, targets), 0) + base
    share = jnp.zeros((targets, targets), jnp.float32)
    for corner in range(4):
        share = share + jnp.where(conn_ref[corner : corner + 1, :] == vertex, 0.25, 0.0)
    for k in range(1, rows):
        source_copy(k).wait_recv()
    both = recv_source[0 : 2 * part, :]
    for r in range(1, rows):
        both = both + recv_source[r * 2 * part : (r + 1) * 2 * part, :]
    objective = both[part : part + 1, 0:1] / (freqs * points * rows) + 1e-06
    obj_out[...] = objective
    source = unpack(both[0:part, :] / objective, 0)
    low = wide < freqs
    inv_own = pltpu.roll(mine, LANES - inv_at, 1)
    inv_turn = jnp.where(low, -pltpu.roll(inv_own, LANES - freqs, 1), pltpu.roll(inv_own, freqs, 1))
    real = jnp.where(low, source, pltpu.roll(source, freqs, 1))
    imag = jnp.where(low, pltpu.roll(source, LANES - freqs, 1), source)
    mu = jnp.where(wide < 2 * freqs, real * inv_own + imag * inv_turn, 0.0)
    packed = pack(mu)
    mu_row, mu_col = slot(row, part, part), slot(col, part, part)
    mu_src_pack[mu_row, :] = packed
    mu_tgt_pack[mu_col, :] = packed
    mu_copies = [
        push(2, mu_src_pack.at[mu_row], mu_src_pack.at[mu_row], row_peer(k), row_sems, k)
        for k in range(rows - 1, 0, -1)
    ] + [
        push(2, mu_tgt_pack.at[mu_col], mu_tgt_pack.at[mu_col], col_peer(k), col_sems, k)
        for k in range(1, cols)
    ]
    square_buf[0:own, :] = mu
    both_out[0 : 2 * freqs, :] = jnp.transpose(square_buf[...])[0 : 2 * freqs, 0:own]
    def open_mu(packs, opened):
        def open_step(block, carry):
            opened[slot(block, own, own), :] = unpack(packs[slot(block, part, part), :], 0)
            return carry

        return open_step

    for copy in mu_copies[rows - 1 :]:
        copy.wait_recv()
    lax.fori_loop(0, cols, open_mu(mu_tgt_pack, mu_tgt), 0)
    if keep:

        def first_step(step, carry):
            span = pl.ds(pl.multiple_of(step * STEP, STEP), STEP)
            tmu = mu_tgt[span, :]
            weight = jnp.zeros((STEP, sources), jnp.float32)
            for f in range(freqs):
                g = freqs + f
                tm_real, tm_imag = tmu[:, f : f + 1], tmu[:, g : g + 1]
                weight = weight + (tm_real * deriv_re[f, span, :] - tm_imag * deriv_im[f, span, :])
            weight_buf[span, :] = weight
            return carry

        lax.fori_loop(0, targets // STEP, first_step, 0)
    for copy in mu_copies[: rows - 1]:
        copy.wait_recv()
    lax.fori_loop(0, rows, open_mu(mu_src_pack, mu_src), 0)
    mu_rows[...] = jnp.transpose(mu_src[...])
    scale = 1.0 / math.sqrt(sources * cols * freqs)
    lane = lax.broadcasted_iota(jnp.int32, (STEP, LANES), 1)

    def sens_step(step, carry):
        span = pl.ds(pl.multiple_of(step * STEP, STEP), STEP)
        block, tmu = tgt_buf[span, :], mu_tgt[span, :]
        offset = gaps(block)
        distance, inverse = lengths(offset)
        weight = weight_buf[span, :] if keep else jnp.zeros((STEP, sources), jnp.float32)
        for f in range(freqs):
            g = freqs + f
            sm_real, sm_imag = mu_rows[f : f + 1, :], mu_rows[g : g + 1, :]
            if keep:
                weight = weight + (sm_real * turned_re[f, span, :] - sm_imag * turned_im[f, span, :])
                continue
            der_real, der_imag = derivative(f, distance, inverse)
            tm_real, tm_imag = tmu[:, f : f + 1], tmu[:, g : g + 1]
            t_real, t_imag = block[:, f : f + 1], block[:, g : g + 1]
            s_real, s_imag = src_rows[f : f + 1, :], src_rows[g : g + 1, :]
            prod_real = tm_real * s_real - tm_imag * s_imag + sm_real * t_real - sm_imag * t_imag
            prod_imag = tm_real * s_imag + tm_imag * s_real + sm_real * t_imag + sm_imag * t_real
            weight = weight + (prod_real * der_real - prod_imag * der_imag)
        total = jnp.zeros((STEP, LANES), jnp.float32)
        for axis in range(3):
            part = jnp.sum(weight * offset[axis], axis=1, keepdims=True)
            total = jnp.where(lane == axis, part * scale, total)
        sens_buf[span, :] = total
        return carry

    lax.fori_loop(0, targets // STEP, sens_step, 0)
    vert_send[...] = lax.dot_general(
        jnp.transpose(sens_buf[...])[0:8, :],
        share,
        (((1,), (1,)), ((), ())),
        preferred_element_type=jnp.float32,
        precision=lax.Precision.HIGHEST,
    )
    per_group = LANES // own

    def vert_group(c):
        start = lax.div(c, per_group) * LANES
        return vert_send.at[:, pl.ds(pl.multiple_of(start, LANES), LANES)]

    vert_mine = slot(col, 8, 8)
    vert_copies = [
        push(
            3, vert_group(lax.rem(col + k, cols)), vert_recv.at[vert_mine], col_peer(k), col_sems, k
        )
        for k in range(1, cols)
    ]
    vert_recv[vert_mine, :] = vert_group(col)[...]
    for copy in vert_copies:
        copy.wait_recv()
    total = vert_recv[0:8, :]
    for k in range(1, cols):
        total = total + vert_recv[k * 8 : (k + 1) * 8, :]
    place_in = lax.rem(col, per_group)
    vertex_own = total
    for spot in range(1, per_group):
        vertex_own = jnp.where(place_in == spot, pltpu.roll(total, LANES - spot * own, 1), vertex_own)
    both_out[2 * freqs :, :] = vertex_own[0:8, 0:own]
    for copy in side + eta_copies + mu_copies + vert_copies:
        copy.wait_send()
    for k in range(1, rows):
        panel_copy(k).wait_send()
        source_copy(k).wait_send()


def on_device(centroids, strengths, self_inv, wavenumbers, field_pos, targets, lists, connect):
    own = centroids.shape[1]
    rows, cols = lax.axis_size("row"), lax.axis_size("col")
    freqs = wavenumbers.shape[0]
    points, listed = lists.shape
    pack_rows = 2 * own * 2 * freqs // LANES
    sources, block = rows * own, cols * own
    keep = freqs * block * sources * 8 <= 16 * 2**20
    kept = (freqs, block, sources) if keep else (1, 8, LANES)
    f32 = jnp.float32
    vmem = pl.BlockSpec(memory_space=pltpu.VMEM)
    hbm = pl.BlockSpec(memory_space=pltpu.HBM)
    smem = pl.BlockSpec(memory_space=pltpu.SMEM)
    both, objective = pl.pallas_call(
        functools.partial(kernel, (rows, cols, own, freqs, points, listed, keep)),
        out_shape=(
            jax.ShapeDtypeStruct((2 * freqs + 8, own), f32),
            jax.ShapeDtypeStruct((1, 1), f32),
        ),
        in_specs=[hbm, hbm, hbm, smem, hbm, hbm, hbm, hbm],
        out_specs=(vmem, vmem),
        scratch_shapes=[
            pltpu.VMEM((LANES, LANES), f32),
            pltpu.VMEM((rows * pack_rows, LANES), f32),
            pltpu.VMEM((cols * pack_rows, LANES), f32),
            pltpu.VMEM((sources, LANES), f32),
            pltpu.VMEM((block, LANES), f32),
            pltpu.VMEM((LANES, sources), f32),
            pltpu.VMEM((listed, points), f32),
            pltpu.VMEM((sources, points), f32),
            pltpu.VMEM((freqs, sources, points), f32),
            pltpu.VMEM((freqs, sources, points), f32),
            pltpu.VMEM((2 * freqs, 8, points), f32),
            pltpu.VMEM((cols, 2 * freqs, points), f32),
            pltpu.VMEM((2 * freqs, points), f32),
            pltpu.VMEM((rows * pack_rows, LANES), f32),
            pltpu.VMEM((rows * pack_rows, LANES), f32),
            pltpu.VMEM((rows * pack_rows // 2, LANES), f32),
            pltpu.VMEM((cols * pack_rows // 2, LANES), f32),
            pltpu.VMEM((sources, LANES), f32),
            pltpu.VMEM((block, LANES), f32),
            pltpu.VMEM((LANES, sources), f32),
            pltpu.VMEM(kept, f32),
            pltpu.VMEM(kept, f32),
            pltpu.VMEM(kept, f32),
            pltpu.VMEM(kept, f32),
            pltpu.VMEM(kept[1:], f32),
            pltpu.VMEM((block, LANES), f32),
            pltpu.VMEM((8, block), f32),
            pltpu.VMEM((cols * 8, LANES), f32),
            pltpu.SemaphoreType.DMA((3, rows)),
            pltpu.SemaphoreType.DMA((3, rows)),
            pltpu.SemaphoreType.DMA((4, cols)),
            pltpu.SemaphoreType.DMA((4, cols)),
            pltpu.VMEM(centroids.shape, f32),
            pltpu.VMEM(strengths.shape, f32),
            pltpu.VMEM(self_inv.shape, f32),
            pltpu.VMEM(field_pos.shape, f32),
            pltpu.VMEM(targets.shape, f32),
            pltpu.VMEM((listed, points), jnp.int32),
            pltpu.VMEM(connect.shape, jnp.int32),
            pltpu.SemaphoreType.DMA((7,)),
        ],
        compiler_params=pltpu.CompilerParams(
            collective_id=0, has_side_effects=True, vmem_limit_bytes=60 * 2**20
        ),
    )(centroids, strengths, self_inv, wavenumbers, field_pos, targets, lists.T, connect)
    return both[: 2 * freqs], both[2 * freqs : 2 * freqs + 3], objective.reshape(())


def solution(mesh):
    return jax.shard_map(
        on_device,
        mesh=mesh,
        in_specs=(
            P(None, ("row", "col")),
            P(None, ("row", "col")),
            P(None, ("row", "col")),
            P(),
            P(None, "row"),
            P(None, "row"),
            P("row", None),
            P(None, "row"),
        ),
        out_specs=(P(None, ("row", "col")), P(None, ("row", "col")), P()),
        check_vma=False,
    )
```
